256 devices in a mesh: tm: 64 (over y, x_lo, z), clip: 4 (over x_hi, core).
Axes of the slice: x: 4 (x_hi: 2, x_lo: 2; x = x_hi * 2 + x_lo), y: 4, z: 8, core: 2. Of those that a mesh axis runs over, the one named last changes fastest.
Arguments:
- frames: bfloat16 [8, 128, 64, 1024], P('clip', 'tm'), may hold values from -6 to 6
- vis_pos: int32 [64], replicated, may hold values from 0 to 783, as said below
- conv_weight: float32 [27, 1024], replicated, may hold values from -0.5 to 0.5
- norm_gain: float32 [1024], replicated, may hold values from 0.5 to 1.5
- qkv_weight: bfloat16 [1024, 1536], replicated, may hold values from -0.1875 to 0.1875
- out_weight: bfloat16 [512, 1024], replicated, may hold values from -0.25 to 0.25
- out_grad: bfloat16 [8, 128, 64, 1024], P('clip', 'tm'), may hold values from -6 to 6
Outputs:
- block_out: bfloat16 [8, 128, 64, 1024], P('clip', 'tm')
- grad_qkv: float32 [1024, 1536], P('tm')
- grad_out: float32 [512, 1024], P(None, 'tm')
- grad_conv: float32 [27, 1024], P(None, 'tm')
- grad_gain: float32 [1024], P('tm')
The draws below stay inside these ranges and needn't reach their ends.
Inputs may be any that keep to these rules, and one draw needn't show every extreme that they name: `vis_pos`: 64 distinct positions in rising order.
All inputs are finite; a program needn't handle non-finite values.
Results may differ from the reference program's by a relative error of at most 0.0095.
Values may be sent and summed in bfloat16 or wider, within the bound.
No kernel may reach another device: no remote copies, remote signals or barrier semaphores. Data moves between devices by JAX's collectives and lax.ppermute only.
A program may use at most 128 MiB of HBM per device.

```python
import jax
import jax.numpy as jnp
from jax import lax

D = 1024
HEADS = 8
HDIM = 64
VIS = 64
GRID = 28
FRAMES = 128
CLIPS = 8


def draw_vis_pos(key, part):
    order = jax.random.permutation(key, GRID * GRID)
    return jnp.sort(order[:VIS]).astype(jnp.int32)


def levels(key, dims, shards, smallest, top_value):
    factor_of, own = 1.0, jax.random.fold_in(key, 6)
    for axis_at, blocks in shards:
        steps = jnp.exp(jax.random.uniform(jax.random.fold_in(own, axis_at), (blocks,), jnp.float32, smallest / len(shards), top_value / len(shards)))
        factor_of = factor_of * jnp.repeat(steps, dims[axis_at] // blocks).reshape([-1 if axis == axis_at else 1 for axis in range(len(dims))])
    return factor_of


def bell_draw(stream_key, extent, spread, most, split=(), dtype=jnp.bfloat16):
    result = jax.random.normal(stream_key, extent, jnp.float32) * spread
    if len(split) > 0:
        result = levels(stream_key, extent, split, -0.22, 0.18) * result
    return jnp.clip(result, min=-most, max=most).astype(dtype)


def setup_inputs(seed: int = 0) -> dict:
    seeds = jax.random.split(jax.random.key(seed), 8)
    return {
        "frames": bell_draw(seeds[0], (CLIPS, FRAMES, VIS, D), 1.0, 6.0, ((0, 4), (1, 64))),
        "vis_pos": draw_vis_pos(jax.random.fold_in(seeds[7], 71), 0),
        "conv_weight": jnp.clip(jax.random.uniform(seeds[2], (27, D), jnp.float32, -0.5, 0.5), -0.5, 0.5),
        "norm_gain": jnp.clip(1.0 + 0.1 * jax.random.normal(seeds[3], (D,), jnp.float32), 0.5, 1.5),
        "qkv_weight": bell_draw(seeds[4], (D, 3 * HEADS * HDIM), D ** -0.5, 0.1875),
        "out_weight": bell_draw(seeds[5], (HEADS * HDIM, D), (HEADS * HDIM) ** -0.5, 0.25),
        "out_grad": bell_draw(seeds[6], (CLIPS, FRAMES, VIS, D), 1.0, 6.0, ((0, 4), (1, 64))),
    }


EPSILON = 1e-05
SCORE_SCALE = 0.125

def tap_matrices(vis_pos):
    row_of = vis_pos // GRID
    col_of = vis_pos % GRID
    mats = []
    for row_step in (-1, 0, 1):
        for col_step in (-1, 0, 1):
            match = (row_of[None, :] == row_of[:, None] + row_step) & (col_of[None, :] == col_of[:, None] + col_step)
            mats.append(match)
    return jnp.stack(mats).astype(jnp.bfloat16)

def attend(queries, key_part, value_part):
    scores = jnp.einsum('cfphe,cgphe->cphfg', queries.astype(jnp.float32), key_part.astype(jnp.float32)) * SCORE_SCALE
    weights = jnp.exp(scores)
    weights = weights / lax.optimization_barrier(jnp.sum(weights, axis=-1, keepdims=True))
    weights = lax.optimization_barrier(weights.astype(jnp.bfloat16))
    attended = jnp.einsum('cphfg,cgphe->cfphe', weights.astype(jnp.float32), value_part.astype(jnp.float32))
    return attended.astype(jnp.bfloat16)

def clip_pass(frame_toks, grad_toks, tap_mats, conv_weight, norm_gain, qkv_weight, out_weight):
    inner = HEADS * HDIM
    zero_frame = jnp.zeros((1, VIS, D), jnp.bfloat16)
    padded = jnp.concatenate([zero_frame, frame_toks, zero_frame], axis=0)
    conv = jnp.zeros((FRAMES, VIS, D), jnp.float32)
    shifted = []
    for offset in range(9):
        moved = jnp.einsum('ij,tjd->tid', tap_mats[offset].astype(jnp.float32), padded.astype(jnp.float32)).astype(jnp.bfloat16)
        shifted.append(moved)
        for lag in range(3):
            conv = conv + conv_weight[lag * 9 + offset] * moved[lag:lag + FRAMES].astype(jnp.float32)
    mixed_in = frame_toks.astype(jnp.float32) + conv
    average = lax.optimization_barrier(jnp.mean(mixed_in, axis=-1, keepdims=True))
    centred = mixed_in - average
    variance = lax.optimization_barrier(jnp.mean(centred * centred, axis=-1, keepdims=True))
    inv_std = lax.rsqrt(variance + EPSILON)
    normed = centred * inv_std
    hidden = (normed * norm_gain).astype(jnp.bfloat16)
    flat_hidden = hidden.reshape(FRAMES * VIS, D)
    qkv = jnp.dot(flat_hidden, qkv_weight, preferred_element_type=jnp.float32).astype(jnp.bfloat16)
    unpacked = qkv.reshape(1, FRAMES, VIS, 3, HEADS, HDIM)
    flat_grad = grad_toks.reshape(FRAMES * VIS, D)
    attn_grad = jnp.dot(flat_grad, out_weight.T, preferred_element_type=jnp.float32).astype(jnp.bfloat16)
    attended, backward = jax.vjp(attend, unpacked[:, :, :, 0], unpacked[:, :, :, 1], unpacked[:, :, :, 2])
    grad_parts = backward(attn_grad.reshape(1, FRAMES, VIS, HEADS, HDIM))
    grad_packed = jnp.stack(grad_parts, axis=3).reshape(FRAMES * VIS, 3 * inner)
    flat_attn = attended.reshape(FRAMES * VIS, inner)
    proj = jnp.dot(flat_attn, out_weight, preferred_element_type=jnp.float32)
    block_out = (mixed_in + proj.reshape(FRAMES, VIS, D)).astype(jnp.bfloat16)
    grad_out = jnp.dot(flat_attn.T, flat_grad, preferred_element_type=jnp.float32)
    grad_qkv = jnp.dot(flat_hidden.T, grad_packed, preferred_element_type=jnp.float32)
    grad_hidden = jnp.dot(grad_packed, qkv_weight.T, preferred_element_type=jnp.float32).reshape(FRAMES, VIS, D)
    grad_gain = lax.optimization_barrier(jnp.sum(grad_hidden * normed, axis=(0, 1)))
    scaled = grad_hidden * norm_gain
    grad_mixed = inv_std * (scaled - lax.optimization_barrier(jnp.mean(scaled, axis=-1, keepdims=True)) - normed * lax.optimization_barrier(jnp.mean(scaled * normed, axis=-1, keepdims=True))) + grad_toks.astype(jnp.float32)
    conv_rows = []
    for lag in range(3):
        for offset in range(9):
            conv_rows.append(lax.optimization_barrier(jnp.sum(grad_mixed * shifted[offset][lag:lag + FRAMES].astype(jnp.float32), axis=(0, 1))))
    grad_conv = jnp.stack(conv_rows)
    return (block_out, grad_qkv, grad_out, grad_conv, grad_gain)

def reference(frames, vis_pos, conv_weight, norm_gain, qkv_weight, out_weight, out_grad):
    tap_mats = tap_matrices(vis_pos)

    def one_clip(pair):
        return clip_pass(pair[0], pair[1], tap_mats, conv_weight, norm_gain, qkv_weight, out_weight)
    block_out, grad_qkv, grad_out, grad_conv, grad_gain = lax.map(one_clip, (frames, out_grad))
    return (block_out, lax.optimization_barrier(jnp.sum(grad_qkv, axis=0)), lax.optimization_barrier(jnp.sum(grad_out, axis=0)), lax.optimization_barrier(jnp.sum(grad_conv, axis=0)), lax.optimization_barrier(jnp.sum(grad_gain, axis=0)))
```

```python
import jax
import jax.numpy as jnp
from jax import lax
from jax.experimental import pallas as pl
from jax.experimental.pallas import tpu as pltpu
from jax.sharding import PartitionSpec as P

HEADS = 8
HDIM = 64
GRID = 28
EPSILON = 1e-05
SCORE_SCALE = 0.125
F32 = jnp.float32
BF16 = jnp.bfloat16
VMEM_BYTES = 56 * 1024 * 1024

WIDTH = 1024
INNER = HEADS * HDIM
VIS = 64
CHUNK = 256
STEPS = [(a, b) for a in (-1, 0, 1) for b in (-1, 0, 1)]
SIDES = [s for s in range(9) if s != 4]


def call(kernel, out_shape, scratch=(), cost=None):
    def run(*args, smem=0):
        specs = [pl.BlockSpec(memory_space=pltpu.SMEM)] * smem
        specs += [pl.BlockSpec(memory_space=pltpu.VMEM)] * (len(args) - smem)
        return pl.pallas_call(
            kernel,
            out_shape=out_shape,
            in_specs=specs,
            out_specs=jax.tree.map(lambda _: pl.BlockSpec(memory_space=pltpu.VMEM), out_shape),
            scratch_shapes=list(scratch),
            compiler_params=pltpu.CompilerParams(vmem_limit_bytes=VMEM_BYTES),
            cost_estimate=cost,
            name=kernel.__name__,
        )(*args)

    return run


def shape(dims, dtype):
    return jax.ShapeDtypeStruct(dims, dtype)


def mm(left, right):
    return jnp.dot(left, right, preferred_element_type=F32)


def mm_nt(left, right):
    return lax.dot_general(left, right, (((1,), (1,)), ((), ())), preferred_element_type=F32)


def mm_tn(left, right):
    return lax.dot_general(left, right, (((0,), (0,)), ((), ())), preferred_element_type=F32)


def swap_matrix():
    row = lax.broadcasted_iota(jnp.int32, (256, 256), 0)
    col = lax.broadcasted_iota(jnp.int32, (256, 256), 1)
    hit = (row >> 4) + ((row & 15) << 4) == col
    return jnp.where(hit, 1.0, 0.0).astype(BF16)


def tap_rows(pos_col, pos_row):
    def key(pos):
        return pos + 36 * ((pos * 2341) >> 16)

    diff = key(pos_row) - key(pos_col)
    mats = [jnp.where(diff == 64 * STEPS[s][0] + STEPS[s][1], 1.0, 0.0) for s in SIDES]
    return jnp.concatenate(mats, axis=0).astype(BF16)


def norm_parts(mixed):
    average = jnp.mean(mixed, axis=-1, keepdims=True)
    centred = mixed - average
    variance = jnp.mean(centred * centred, axis=-1, keepdims=True)
    inv_std = lax.rsqrt(variance + EPSILON)
    return centred * inv_std, inv_std


def frame_at(frames_ref, head_ref, tail_ref, c, u, cols):
    if u == 0:
        return head_ref[c, 0, :, cols]
    if u == 3:
        return tail_ref[c, 0, :, cols]
    return frames_ref[c, u - 1, :, cols]


def moved_at(taps, cells):
    moved = mm(taps, cells)
    out = [moved[64 * k : 64 * k + 64] for k in range(8)]
    out.insert(4, cells.astype(F32))
    return out


def pack(swap, source, out_ref):
    for b in range(4):
        rows = [source(q, ct, b) for q in range(4) for ct in range(4)]
        moved = mm(swap, jnp.concatenate(rows, axis=0)).astype(BF16)
        out_ref[16 * b : 16 * b + 16] = moved.reshape(16, 16, moved.shape[-1])


def unpack(swap, in_ref, sink):
    for b in range(4):
        block = in_ref[16 * b : 16 * b + 16]
        moved = mm(swap, block.reshape(256, block.shape[-1])).astype(BF16)
        for q in range(4):
            for ct in range(4):
                at = 16 * (4 * q + ct)
                sink(q, ct, b, moved[at : at + 16])


def mix_kernel(
    frames_ref, head_ref, tail_ref, pos_col, pos_row, w_ref, gain_ref, grad_ref,
    send_ref, mixed_ref, hidden_ref,
):
    taps = tap_rows(pos_col[...], pos_row[...])

    @pl.loop(0, WIDTH // CHUNK)
    def _(n):
        cols = pl.ds(pl.multiple_of(n * CHUNK, CHUNK), CHUNK)
        w = w_ref[:, cols]
        for c in range(2):
            acc = [frames_ref[c, t, :, cols].astype(F32) for t in range(2)]
            for u in range(4):
                moved = moved_at(taps, frame_at(frames_ref, head_ref, tail_ref, c, u, cols))
                for s in range(9):
                    for t in range(2):
                        lag = u - t
                        if 0 <= lag <= 2:
                            at = 9 * lag + s
                            acc[t] = acc[t] + w[at : at + 1] * moved[s]
            for t in range(2):
                at = 64 * (2 * c + t)
                mixed_ref[at : at + 64, cols] = acc[t]

    for k in range(8):
        rows = slice(32 * k, 32 * k + 32)
        normed, _ = norm_parts(mixed_ref[rows])
        hidden_ref[rows] = (normed * gain_ref[...]).astype(BF16)

    def source(q, ct, b):
        if q < 2:
            return hidden_ref[64 * ct + 16 * b : 64 * ct + 16 * b + 16, 512 * q : 512 * q + 512]
        return grad_ref[ct // 2, ct % 2, 16 * b : 16 * b + 16, 512 * (q - 2) : 512 * (q - 2) + 512]

    pack(swap_matrix(), source, send_ref)


def attend_kernel(
    core_ref, recv_ref, wqkv_ref, wout_ref,
    give_ref, keep_ref, tok_ref, attn_ref,
    hidden_ref, grad_ref, qkv_ref, up_ref, part_ref,
):
    def sink(q, ct, b, block):
        target = hidden_ref if q < 2 else grad_ref
        at = 64 * ct + 16 * b
        target[at : at + 16, 512 * (q % 2) : 512 * (q % 2) + 512] = block

    unpack(swap_matrix(), recv_ref, sink)
    for n in range(3):
        cols = slice(512 * n, 512 * n + 512)
        qkv_ref[:, cols] = mm(hidden_ref[...], wqkv_ref[:, cols]).astype(BF16)
    up_ref[...] = mm_nt(grad_ref[...], wout_ref[...]).astype(BF16)

    low = lax.broadcasted_iota(jnp.int32, (128, 128), 1) < 64

    def halves(value):
        zero = jnp.zeros_like(value)
        return jnp.where(low, value, zero), jnp.where(low, zero, value)

    for c in range(2):
        rows = slice(128 * c, 128 * c + 128)
        for p in range(4):
            at = 128 * p
            query = qkv_ref[rows, at : at + 128]
            key = qkv_ref[rows, INNER + at : INNER + at + 128]
            value = qkv_ref[rows, 2 * INNER + at : 2 * INNER + at + 128]
            upstream = up_ref[rows, at : at + 128]
            queries, keys, values, upstreams = (halves(x) for x in (query, key, value, upstream))
            weights, grads = [], []
            for e in range(2):
                scores = mm_nt(queries[e], key) * SCORE_SCALE
                scores = jnp.exp(scores - jnp.max(scores, axis=-1, keepdims=True))
                soft = scores / jnp.sum(scores, axis=-1, keepdims=True)
                weights.append(soft.astype(BF16))
                d_soft = mm_nt(upstreams[e], value).astype(BF16).astype(F32)
                inner = jnp.sum(d_soft * soft, axis=-1, keepdims=True)
                grads.append((soft * (d_soft - inner) * SCORE_SCALE).astype(BF16))
            over_keys = jnp.concatenate(grads, axis=1)
            over_queries = jnp.concatenate(grads, axis=0)
            attn_ref[rows, at : at + 128] = mm(
                jnp.concatenate(weights, axis=1), jnp.concatenate(values, axis=0)
            ).astype(BF16)
            tok_ref[rows, at : at + 128] = mm(over_keys, jnp.concatenate(keys, axis=0)).astype(BF16)
            tok_ref[rows, INNER + at : INNER + at + 128] = mm_tn(
                over_queries, jnp.concatenate(queries, axis=0)
            ).astype(BF16)
            tok_ref[rows, 2 * INNER + at : 2 * INNER + at + 128] = mm_tn(
                jnp.concatenate(weights, axis=0), jnp.concatenate(upstreams, axis=0)
            ).astype(BF16)

    for n in range(3):
        cols = slice(512 * n, 512 * n + 512)
        part_ref[:, cols] = mm_tn(hidden_ref[...], tok_ref[:, cols]).astype(BF16)
    part_ref[:, 1536:] = mm_tn(grad_ref[...], attn_ref[...]).astype(BF16)
    core = core_ref[0]
    keep_ref[...] = part_ref[:, pl.ds(pl.multiple_of(core * 1024, 1024), 1024)]
    give_ref[...] = part_ref[:, pl.ds(pl.multiple_of((1 - core) * 1024, 1024), 1024)]


def return_kernel(tok_ref, attn_ref, wqkv_ref, send_ref, back_ref):
    for n in range(2):
        cols = slice(512 * n, 512 * n + 512)
        back_ref[:, cols] = mm_nt(tok_ref[...], wqkv_ref[cols, :]).astype(BF16)
    back_ref[:, WIDTH:] = attn_ref[...]

    def source(q, ct, b):
        return back_ref[64 * ct + 16 * b : 64 * ct + 16 * b + 16, 384 * q : 384 * q + 384]

    pack(swap_matrix(), source, send_ref)


def finish_kernel(
    frames_ref, head_ref, tail_ref, pos_col, pos_row, gain_ref, grad_ref, wout_ref, mixed_ref, recv_ref,
    out_ref, small_ref,
    back_ref, gm_ref, rows_ref,
):
    def sink(q, ct, b, block):
        back_ref[64 * ct + 16 * b : 64 * ct + 16 * b + 16, 384 * q : 384 * q + 384] = block

    unpack(swap_matrix(), recv_ref, sink)
    gain = gain_ref[...]
    rows_ref[...] = jnp.zeros_like(rows_ref)
    for ct in range(4):
        at = slice(64 * ct, 64 * ct + 64)
        proj = mm(back_ref[at, WIDTH:], wout_ref[...])
        out_ref[ct // 2, ct % 2] = (mixed_ref[at] + proj).astype(BF16)
    gain_sum = jnp.zeros((8, WIDTH), F32)
    for k in range(8):
        rows = slice(32 * k, 32 * k + 32)
        normed, inv_std = norm_parts(mixed_ref[rows])
        grad_hidden = back_ref[rows, :WIDTH].astype(F32)
        prod = grad_hidden * normed
        gain_sum = gain_sum + jnp.sum(prod.reshape(4, 8, WIDTH), axis=0)
        scaled = grad_hidden * gain
        first = jnp.mean(scaled, axis=-1, keepdims=True)
        second = jnp.mean(prod * gain, axis=-1, keepdims=True)
        ct, half = k // 2, k % 2
        upstream = grad_ref[ct // 2, ct % 2, 32 * half : 32 * half + 32, :].astype(F32)
        gm_ref[rows] = inv_std * (scaled - first - normed * second) + upstream
    rows_ref[27:28, :] = jnp.sum(gain_sum, axis=0, keepdims=True)
    taps = tap_rows(pos_col[...], pos_row[...])

    @pl.loop(0, WIDTH // CHUNK)
    def _(n):
        cols = pl.ds(pl.multiple_of(n * CHUNK, CHUNK), CHUNK)
        acc = [jnp.zeros((8, CHUNK), F32) for _ in range(27)]
        for c in range(2):
            gm = [gm_ref[64 * (2 * c + t) : 64 * (2 * c + t) + 64, cols] for t in range(2)]
            for u in range(4):
                moved = moved_at(taps, frame_at(frames_ref, head_ref, tail_ref, c, u, cols))
                for s in range(9):
                    for t in range(2):
                        lag = u - t
                        if 0 <= lag <= 2:
                            prod = (gm[t] * moved[s]).reshape(8, 8, CHUNK)
                            acc[9 * lag + s] = acc[9 * lag + s] + jnp.sum(prod, axis=0)
        for at in range(27):
            rows_ref[at : at + 1, cols] = jnp.sum(acc[at], axis=0, keepdims=True)

    small_ref[...] = jnp.transpose(rows_ref[...]).astype(BF16)


def core_sum_kernel(place_ref, keep_ref, got_ref, *piece_refs):
    x_lo, x_hi = place_ref[0], place_ref[1]
    for piece, (flip_lo, flip_hi) in enumerate(((0, 0), (1, 0), (0, 1), (1, 1))):
        lo = x_lo if flip_lo == 0 else 1 - x_lo
        hi = x_hi if flip_hi == 0 else 1 - x_hi
        cols = pl.ds(pl.multiple_of(hi * 512, 512), 512)
        for y in range(4):
            rows = pl.ds(pl.multiple_of(256 * y + 128 * lo, 128), 128)
            both = keep_ref[rows, cols].astype(F32) + got_ref[rows, cols].astype(F32)
            piece_refs[piece][y] = both.astype(BF16)


def x_sum_kernel(place_ref, a_ref, b_ref, c_ref, d_ref, *piece_refs):
    y = place_ref[0]
    for k in range(4):
        at = (y + k) & 3
        total = a_ref[at].astype(F32) + b_ref[at].astype(F32)
        total = total + (c_ref[at].astype(F32) + d_ref[at].astype(F32))
        piece_refs[k][...] = total.astype(BF16)


def y_sum_kernel(a_ref, b_ref, c_ref, d_ref, small_ref, out_ref):
    total = a_ref[...].astype(F32) + b_ref[...].astype(F32)
    total = total + (c_ref[...].astype(F32) + d_ref[...].astype(F32))
    out_ref[:, :, :512] = total.astype(BF16).reshape(8, 16, 512)
    small = jnp.sum(small_ref[...].astype(F32), axis=0)
    out_ref[:, :, 512:] = small.astype(BF16).reshape(8, 16, 128)


def z_sum_kernel(recv_ref, out_ref):
    out_ref[...] = jnp.sum(recv_ref[...].astype(F32), axis=0)


def last_kernel(place_ref, own_ref, core_ref, hi_ref, both_ref, qkv_ref, out_ref, small_ref, full_ref):
    x_hi, core = place_ref[0], place_ref[1]
    refs = ((own_ref, 0, 0), (core_ref, 0, 1), (hi_ref, 1, 0), (both_ref, 1, 1))
    for ref, flip_hi, flip_core in refs:
        hi = x_hi if flip_hi == 0 else 1 - x_hi
        co = core if flip_core == 0 else 1 - core
        at = pl.multiple_of(1024 * co + 512 * hi, 512)
        full_ref[:, pl.ds(at, 512)] = ref[:, :512]
    qkv_ref[...] = full_ref[:, :1536]
    out_ref[...] = jnp.transpose(full_ref[:, 1536:])
    small = own_ref[:, 512:] + core_ref[:, 512:] + (hi_ref[:, 512:] + both_ref[:, 512:])
    small_ref[...] = jnp.transpose(small)


def flip(tm_bits, clip_bits):
    pairs = [(t * 4 + k, (t ^ tm_bits) * 4 + (k ^ clip_bits)) for t in range(64) for k in range(4)]
    return lambda value: lax.ppermute(value, ("tm", "clip"), pairs)


def body(frames, vis_pos, conv_weight, norm_gain, qkv_weight, out_weight, out_grad):
    ends = lax.axis_size("tm") - 1
    tm, clip = lax.axis_index("tm"), lax.axis_index("clip")
    y, x_lo = tm // 16, (tm // 8) % 2
    x_hi, core = clip // 2, clip % 2

    def scalars(*values):
        return jnp.stack(values).astype(jnp.int32)

    head = lax.ppermute(frames[:, 1:], "tm", [(i, i + 1) for i in range(ends)])
    tail = lax.ppermute(frames[:, :1], "tm", [(i + 1, i) for i in range(ends)])
    pos_col, pos_row = vis_pos.reshape(VIS, 1), vis_pos.reshape(1, VIS)
    gain = norm_gain.reshape(1, WIDTH)
    send, mixed = call(
        mix_kernel,
        (shape((64, 16, 512), BF16), shape((256, WIDTH), F32)),
        [pltpu.VMEM((256, WIDTH), BF16)],
    )(frames, head, tail, pos_col, pos_row, conv_weight, gain, out_grad)
    recv = lax.all_to_all(send, "tm", 0, 0, tiled=True)
    give, keep, tok, attn = call(
        attend_kernel,
        (
            shape((1024, 1024), BF16),
            shape((1024, 1024), BF16),
            shape((256, 3 * INNER), BF16),
            shape((256, INNER), BF16),
        ),
        [
            pltpu.VMEM((256, WIDTH), BF16),
            pltpu.VMEM((256, WIDTH), BF16),
            pltpu.VMEM((256, 3 * INNER), BF16),
            pltpu.VMEM((256, INNER), BF16),
            pltpu.VMEM((1024, 2048), BF16),
        ],
    )(scalars(core), recv, qkv_weight, out_weight, smem=1)
    got = flip(0, 1)(give)
    back = call(
        return_kernel, shape((64, 16, 384), BF16), [pltpu.VMEM((256, 1536), BF16)]
    )(tok, attn, qkv_weight)
    pieces = call(core_sum_kernel, (shape((4, 128, 512), BF16),) * 4)(
        scalars(x_lo, x_hi), keep, got, smem=1
    )
    back, pieces = lax.optimization_barrier((back, pieces))
    crossed = (flip(8, 0)(pieces[1]), flip(0, 2)(pieces[2]), flip(8, 2)(pieces[3]))
    back_recv = lax.all_to_all(back, "tm", 0, 0, tiled=True)
    parts = call(x_sum_kernel, (shape((128, 512), BF16),) * 4)(
        scalars(y), pieces[0], *crossed, smem=1
    )
    turned = [
        lax.ppermute(parts[k], "tm", [(i, (i + 16 * k) % 64) for i in range(64)]) for k in (1, 2, 3)
    ]
    block_out, small = call(
        finish_kernel,
        (shape(frames.shape, BF16), shape((1024, 128), BF16)),
        [
            pltpu.VMEM((256, 1536), BF16),
            pltpu.VMEM((256, WIDTH), F32),
            pltpu.VMEM((128, WIDTH), F32),
        ],
    )(frames, head, tail, pos_col, pos_row, gain, out_grad, out_weight, mixed, back_recv)
    yx_groups = [[16 * b + 8 * a + z for b in range(4) for a in range(2)] for z in range(8)]
    z_groups = [[8 * g + z for z in range(8)] for g in range(8)]
    small_recv = lax.all_to_all(
        small.reshape(8, 128, 128), "tm", 0, 0, tiled=True, axis_index_groups=yx_groups
    )
    z_send = call(y_sum_kernel, shape((8, 16, 640), BF16))(parts[0], *turned, small_recv)
    z_recv = lax.all_to_all(z_send, "tm", 0, 0, tiled=True, axis_index_groups=z_groups)
    own = call(z_sum_kernel, shape((16, 640), F32))(z_recv)
    grad_qkv, grad_out, smalls = call(
        last_kernel,
        (shape((16, 1536), F32), shape((512, 16), F32), shape((128, 16), F32)),
        [pltpu.VMEM((16, 2048), F32)],
    )(scalars(x_hi, core), own, flip(0, 1)(own), flip(0, 2)(own), flip(0, 3)(own), smem=1)
    return block_out, grad_qkv, grad_out, smalls[:27], smalls[27]


def solution(mesh):
    return jax.shard_map(
        body,
        mesh=mesh,
        in_specs=(
            P("clip", "tm", None, None),
            P(),
            P(),
            P(),
            P(),
            P(),
            P("clip", "tm", None, None),
        ),
        out_specs=(
            P("clip", "tm", None, None),
            P("tm", None),
            P(None, "tm"),
            P(None, "tm"),
            P("tm"),
        ),
        check_vma=False,
    )
```

```python
import jax
import jax.numpy as jnp
from jax import lax
from jax.experimental import pallas as pl
from jax.experimental.pallas import tpu as pltpu
from jax.sharding import PartitionSpec as P

HEADS = 8
HDIM = 64
GRID = 28
EPSILON = 1e-05
SCORE_SCALE = 0.125
F32 = jnp.float32
BF16 = jnp.bfloat16

WIDTH = 1024
INNER = HEADS * HDIM
VIS = 64
CHUNK = 256
STEPS = [(a, b) for a in (-1, 0, 1) for b in (-1, 0, 1)]
SIDES = [s for s in range(9) if s != 4]


def call(kernel, out_shape, scratch=(), limit=12, streamed=0, cost=None):
    def run(*args):
        def streaming(*refs):
            sources, refs = refs[:streamed], refs[streamed:]
            plain = len(refs) - streamed - 1
            buffers, sems = refs[plain : plain + streamed], refs[-1]
            copies = [
                pltpu.make_async_copy(source, buffer, sems.at[n])
                for n, (source, buffer) in enumerate(zip(sources, buffers))
            ]
            for copy in copies:
                copy.start()
            kernel(lambda n: copies[n].wait(), *buffers, *refs[:plain])

        extra = [pltpu.VMEM(x.shape, x.dtype) for x in args[:streamed]]
        specs = [pl.BlockSpec(memory_space=pltpu.HBM)] * streamed
        specs += [pl.BlockSpec(memory_space=pltpu.VMEM)] * (len(args) - streamed)
        return pl.pallas_call(
            streaming if streamed else kernel,
            out_shape=out_shape,
            in_specs=specs,
            out_specs=jax.tree.map(lambda _: pl.BlockSpec(memory_space=pltpu.VMEM), out_shape),
            scratch_shapes=list(scratch)
            + (extra + [pltpu.SemaphoreType.DMA((streamed,))] if streamed else []),
            compiler_params=pltpu.CompilerParams(vmem_limit_bytes=limit * 1024 * 1024),
            cost_estimate=cost,
            name=kernel.__name__,
        )(*args)

    return run


def shape(dims, dtype):
    return jax.ShapeDtypeStruct(dims, dtype)


def mm(left, right):
    return jnp.dot(left, right, preferred_element_type=F32)


def mm_nt(left, right):
    return lax.dot_general(left, right, (((1,), (1,)), ((), ())), preferred_element_type=F32)


def mm_tn(left, right):
    return lax.dot_general(left, right, (((0,), (0,)), ((), ())), preferred_element_type=F32)


def pack_matrix():
    row = lax.broadcasted_iota(jnp.int32, (256, 256), 0)
    col = lax.broadcasted_iota(jnp.int32, (256, 256), 1)
    return jnp.where(((row & 7) << 5) + (row >> 3) == col, 1.0, 0.0).astype(BF16)


def unpack_matrix():
    row = lax.broadcasted_iota(jnp.int32, (256, 256), 0)
    col = lax.broadcasted_iota(jnp.int32, (256, 256), 1)
    return jnp.where(((row & 31) << 3) + (row >> 5) == col, 1.0, 0.0).astype(BF16)


def tap_rows(pos_row):
    pos = pos_row[...]
    key = pos + 36 * ((pos * 2341) >> 16)
    across = jnp.broadcast_to(key.astype(F32), (VIS, VIS))
    diff = across - jnp.transpose(across)
    mats = [jnp.where(diff == 64 * STEPS[s][0] + STEPS[s][1], 1.0, 0.0) for s in SIDES]
    return jnp.concatenate(mats, axis=0).astype(BF16)


def norm_parts(mixed):
    average = jnp.mean(mixed, axis=-1, keepdims=True)
    centred = mixed - average
    variance = jnp.mean(centred * centred, axis=-1, keepdims=True)
    inv_std = lax.rsqrt(variance + EPSILON)
    return centred * inv_std, inv_std


def frame_at(frames_ref, head_ref, tail_ref, c, u, cols):
    if u == 0:
        return head_ref[c, 0, :, cols]
    if u == 3:
        return tail_ref[c, 0, :, cols]
    return frames_ref[c, u - 1, :, cols]


def moved_at(taps, cells):
    moved = mm(taps, cells)
    out = [moved[64 * k : 64 * k + 64] for k in range(8)]
    out.insert(4, cells.astype(F32))
    return out


def pack(source, out_ref):
    matrix = pack_matrix()
    for b in range(2):
        rows = [source(h, ct, b) for h in range(2) for ct in range(4)]
        moved = mm(matrix, jnp.concatenate(rows, axis=0))
        out_ref[32 * b : 32 * b + 32] = moved.reshape(32, 8, moved.shape[-1]).astype(BF16)


def unpack(in_ref, sink):
    matrix = unpack_matrix()
    for b in range(2):
        block = in_ref[32 * b : 32 * b + 32]
        moved = mm(matrix, block.reshape(256, block.shape[-1])).astype(BF16)
        for h in range(2):
            for ct in range(4):
                at = 32 * (4 * h + ct)
                sink(h, ct, b, moved[at : at + 32])


def unpack_to(in_ref, out_ref):
    width = in_ref.shape[-1]

    def sink(h, ct, b, block):
        at = 64 * ct + 32 * b
        out_ref[at : at + 32, width * h : width * h + width] = block

    unpack(in_ref, sink)


def unpack_two(in_ref, left_ref, right_ref):
    def sink(h, ct, b, block):
        at = 64 * ct + 32 * b
        (left_ref, right_ref)[h][at : at + 32, :] = block

    unpack(in_ref, sink)


def local_kernel(ready, frames_ref, w_ref, grad_ref, pos_row, mixed_ref, rows_ref):
    taps = tap_rows(pos_row)
    ready(0)
    ready(1)

    @pl.loop(0, WIDTH // CHUNK)
    def _(n):
        cols = pl.ds(pl.multiple_of(n * CHUNK, CHUNK), CHUNK)
        w = w_ref[:, cols]
        for c in range(2):
            acc = [frames_ref[c, t, :, cols].astype(F32) for t in range(2)]
            for u in (1, 2):
                moved = moved_at(taps, frames_ref[c, u - 1, :, cols])
                for s in range(9):
                    for t in range(2):
                        at = 9 * (u - t) + s
                        acc[t] = acc[t] + w[at : at + 1] * moved[s]
            for t in range(2):
                at = 64 * (2 * c + t)
                mixed_ref[at : at + 64, cols] = acc[t]

    ready(2)
    for ct in range(4):
        rows_ref[64 * ct : 64 * ct + 64, :] = grad_ref[ct // 2, ct % 2]


def mix_kernel(
    part_ref, rows_ref, head_ref, tail_ref, pos_row, w_ref, gain_ref,
    send_ref, mixed_ref, hidden_ref,
):
    taps = tap_rows(pos_row)

    @pl.loop(0, WIDTH // CHUNK)
    def _(n):
        cols = pl.ds(pl.multiple_of(n * CHUNK, CHUNK), CHUNK)
        w = w_ref[:, cols]
        for c in range(2):
            for t, halo_ref in enumerate((head_ref, tail_ref)):
                moved = moved_at(taps, halo_ref[c, 0, :, cols])
                rows = slice(64 * (2 * c + t), 64 * (2 * c + t) + 64)
                acc = part_ref[rows, cols]
                for s in range(9):
                    at = 18 * t + s
                    acc = acc + w[at : at + 1] * moved[s]
                mixed_ref[rows, cols] = acc

    for k in range(8):
        rows = slice(32 * k, 32 * k + 32)
        normed, _ = norm_parts(mixed_ref[rows])
        hidden_ref[rows] = (normed * gain_ref[...]).astype(BF16)

    def source(h, ct, b):
        return (hidden_ref, rows_ref)[h][64 * ct + 32 * b : 64 * ct + 32 * b + 32, :]

    pack(source, send_ref)


def attend_kernel(
    recv_ref, wqkv_ref, wout_ref,
    send_ref, hidden_ref, grad_ref, tok_ref, attn_ref,
    qkv_ref, up_ref, back_ref,
):
    unpack_two(recv_ref, hidden_ref, grad_ref)
    up_ref[...] = mm_nt(grad_ref[...], wout_ref[...]).astype(BF16)
    for n in range(3):
        cols = slice(512 * n, 512 * n + 512)
        qkv_ref[:, cols] = mm(hidden_ref[...], wqkv_ref[:, cols]).astype(BF16)

    low = lax.broadcasted_iota(jnp.int32, (128, 128), 1) < 64

    def halves(value):
        zero = jnp.zeros_like(value)
        return jnp.where(low, value, zero), jnp.where(low, zero, value)

    for c in range(2):
        rows = slice(128 * c, 128 * c + 128)
        pairs = [slice(128 * p, 128 * p + 128) for p in range(4)]
        query = [qkv_ref[rows, 128 * p : 128 * p + 128] for p in range(4)]
        key = [qkv_ref[rows, INNER + 128 * p : INNER + 128 * p + 128] for p in range(4)]
        value = [qkv_ref[rows, 2 * INNER + 128 * p : 2 * INNER + 128 * p + 128] for p in range(4)]
        upstream = [up_ref[rows, at] for at in pairs]
        queries = [halves(x) for x in query]
        upstreams = [halves(x) for x in upstream]
        heads = [(p, e) for p in range(4) for e in range(2)]
        scores = [mm_nt(queries[p][e], key[p]) * SCORE_SCALE for p, e in heads]
        d_soft = [mm_nt(upstreams[p][e], value[p]).astype(BF16).astype(F32) for p, e in heads]
        scores = [jnp.exp(x - jnp.max(x, axis=-1, keepdims=True)) for x in scores]
        soft = [x / jnp.sum(x, axis=-1, keepdims=True) for x in scores]
        weights = [x.astype(BF16) for x in soft]
        inner = [jnp.sum(d * x, axis=-1, keepdims=True) for d, x in zip(d_soft, soft)]
        grads = [
            (x * (d - i) * SCORE_SCALE).astype(BF16) for d, x, i in zip(d_soft, soft, inner)
        ]
        for p in range(4):
            at = 128 * p
            both = slice(2 * p, 2 * p + 2)
            attn_ref[rows, at : at + 128] = mm(
                jnp.concatenate(weights[both], axis=1), jnp.concatenate(halves(value[p]), axis=0)
            ).astype(BF16)
            tok_ref[rows, at : at + 128] = mm(
                jnp.concatenate(grads[both], axis=1), jnp.concatenate(halves(key[p]), axis=0)
            ).astype(BF16)
            tok_ref[rows, INNER + at : INNER + at + 128] = mm_tn(
                jnp.concatenate(grads[both], axis=0), jnp.concatenate(queries[p], axis=0)
            ).astype(BF16)
            tok_ref[rows, 2 * INNER + at : 2 * INNER + at + 128] = mm_tn(
                jnp.concatenate(weights[both], axis=0), jnp.concatenate(upstreams[p], axis=0)
            ).astype(BF16)

    for n in range(2):
        cols = slice(512 * n, 512 * n + 512)
        back_ref[:, cols] = mm_nt(tok_ref[...], wqkv_ref[cols, :]).astype(BF16)
    back_ref[:, WIDTH:] = attn_ref[...]

    def source(h, ct, b):
        at = 64 * ct + 32 * b
        return back_ref[at : at + 32, 768 * h : 768 * h + 768]

    pack(source, send_ref)


def places():
    tm, clip = lax.axis_index("tm"), lax.axis_index("clip")
    return lax.rem(lax.div(tm, 8), 2), lax.div(tm, 16), lax.div(clip, 2), lax.rem(clip, 2)


def weight_half(hidden_ref, tok_ref, grad_ref, attn_ref, half, sink):
    @pl.when(half == 0)
    def _():
        for n in range(4):
            sink(256 * n, mm_tn(hidden_ref[...], tok_ref[:, 256 * n : 256 * n + 256]))

    @pl.when(half == 1)
    def _():
        for n in range(2):
            sink(256 * n, mm_tn(hidden_ref[...], tok_ref[:, 1024 + 256 * n : 1280 + 256 * n]))
        for n in range(2):
            sink(512 + 256 * n, mm_tn(grad_ref[...], attn_ref[:, 256 * n : 256 * n + 256]))


def part_kernel(hidden_ref, tok_ref, grad_ref, attn_ref, give_ref):
    core = places()[3]

    def sink(at, value):
        give_ref[:, at : at + 256] = value.astype(BF16)

    weight_half(hidden_ref, tok_ref, grad_ref, attn_ref, 1 - core, sink)


def core_sum_kernel(hidden_ref, tok_ref, grad_ref, attn_ref, got_ref, *refs):
    piece_refs, both_ref = refs[:8], refs[8]
    x_lo, y, x_hi, core = places()

    def sink(at, value):
        both = value + got_ref[:, at : at + 256].astype(F32)
        both_ref[:, at : at + 256] = both.astype(BF16)

    weight_half(hidden_ref, tok_ref, grad_ref, attn_ref, core, sink)

    def part(at):
        return both_ref[:, pl.ds(pl.multiple_of(at, 128), 128)]

    for piece, (flip_lo, flip_hi) in enumerate(((0, 0), (1, 0), (0, 1), (1, 1))):
        lo = x_lo if flip_lo == 0 else 1 - x_lo
        hi = x_hi if flip_hi == 0 else 1 - x_hi
        piece_refs[piece][...] = part(256 * hi + 128 * lo)
    for k in range(4):
        piece_refs[4 + k][...] = part(512 + 128 * ((y + k) & 3))


def merge_kernel(*refs):
    out_ref = refs[-1]
    for side in range(2):
        a, b, c, d = (ref[...].astype(F32) for ref in refs[4 * side : 4 * side + 4])
        total = ((a + b) + (c + d)).reshape(64, 16, 128)
        for half in range(2):
            at = 256 * side + 128 * half
            out_ref[:, :, at : at + 128] = total[:, 8 * half : 8 * half + 8].astype(BF16)


def finish_kernel(
    ready, wout_ref, mixed_ref, grad_ref, frames_ref, head_ref, tail_ref, pos_row, gain_ref, recv_ref,
    out_ref, small_ref,
    back_ref, gm_ref, rows_ref,
):
    unpack_to(recv_ref, back_ref)
    gain = gain_ref[...]
    rows_ref[...] = jnp.zeros_like(rows_ref)
    for n in range(6):
        ready(n)
    for ct in range(4):
        at = slice(64 * ct, 64 * ct + 64)
        proj = mm(back_ref[at, WIDTH:], wout_ref[...])
        out_ref[ct // 2, ct % 2] = (mixed_ref[at] + proj).astype(BF16)
    gain_sum = jnp.zeros((8, WIDTH), F32)
    for k in range(8):
        rows = slice(32 * k, 32 * k + 32)
        normed, inv_std = norm_parts(mixed_ref[rows])
        grad_hidden = back_ref[rows, :WIDTH].astype(F32)
        prod = grad_hidden * normed
        gain_sum = gain_sum + jnp.sum(prod.reshape(4, 8, WIDTH), axis=0)
        scaled = grad_hidden * gain
        first = jnp.mean(scaled, axis=-1, keepdims=True)
        second = jnp.mean(prod * gain, axis=-1, keepdims=True)
        ct, half = k // 2, k % 2
        upstream = grad_ref[ct // 2, ct % 2, 32 * half : 32 * half + 32, :].astype(F32)
        gm_ref[rows] = inv_std * (scaled - first - normed * second) + upstream
    rows_ref[27:28, :] = jnp.sum(gain_sum, axis=0, keepdims=True)
    taps = tap_rows(pos_row)

    @pl.loop(0, WIDTH // CHUNK)
    def _(n):
        cols = pl.ds(pl.multiple_of(n * CHUNK, CHUNK), CHUNK)
        acc = [jnp.zeros((8, CHUNK), F32) for _ in range(27)]
        for c in range(2):
            gm = [gm_ref[64 * (2 * c + t) : 64 * (2 * c + t) + 64, cols] for t in range(2)]
            for u in range(4):
                moved = moved_at(taps, frame_at(frames_ref, head_ref, tail_ref, c, u, cols))
                for s in range(9):
                    for t in range(2):
                        lag = u - t
                        if 0 <= lag <= 2:
                            prod = (gm[t] * moved[s]).reshape(8, 8, CHUNK)
                            acc[9 * lag + s] = acc[9 * lag + s] + jnp.sum(prod, axis=0)
        for at in range(27):
            rows_ref[at : at + 1, cols] = jnp.sum(acc[at], axis=0, keepdims=True)

    rows_ref[64:96, :] = rows_ref[0:32, :]
    turned = jnp.transpose(rows_ref[...]).reshape(64, 16, 128)
    left = lax.broadcasted_iota(jnp.int32, (64, 8, 128), 2) < 64
    small_ref[...] = jnp.where(left, turned[:, :8], turned[:, 8:]).astype(BF16)


def tm_sum_kernel(recv_ref, out_ref):
    def over(first, last, at):
        total = recv_ref[first, :, at : at + 128].astype(F32)
        for src in range(first + 1, last):
            total = total + recv_ref[src, :, at : at + 128].astype(F32)
        return total

    for half in range(2):
        rows = slice(8 * half, 8 * half + 8)
        kept = [[over(16 * y + 8 * lo, 16 * y + 8 * lo + 8, 128 * half) for lo in range(2)] for y in range(4)]
        for lo in range(2):
            out_ref[rows, 128 * lo : 128 * lo + 128] = (kept[0][lo] + kept[1][lo]) + (kept[2][lo] + kept[3][lo])
        for y in range(4):
            at = 256 + 128 * y
            out_ref[rows, at : at + 128] = over(16 * y, 16 * y + 16, 256 + 128 * half)
    out_ref[:8, 768:] = over(0, 64, 512)
    out_ref[8:, 768:] = jnp.zeros((8, 128), F32)


def last_kernel(own_ref, core_ref, hi_ref, both_ref, qkv_ref, out_ref, conv_ref, gain_ref, full_ref):
    _, _, x_hi, core = places()
    mine = pl.multiple_of(1024 * core, 1024)
    other = pl.multiple_of(1024 - 1024 * core, 1024)
    here = pl.multiple_of(256 * x_hi, 256)
    there = pl.multiple_of(256 - 256 * x_hi, 256)
    full_ref[:, pl.ds(mine + here, 256)] = own_ref[:, :256]
    full_ref[:, pl.ds(mine + there, 256)] = hi_ref[:, :256]
    full_ref[:, pl.ds(other + here, 256)] = core_ref[:, :256]
    full_ref[:, pl.ds(other + there, 256)] = both_ref[:, :256]
    full_ref[:, pl.ds(mine + 512, 512)] = own_ref[:, 256:768] + hi_ref[:, 256:768]
    full_ref[:, pl.ds(other + 512, 512)] = core_ref[:, 256:768] + both_ref[:, 256:768]
    qkv_ref[...] = full_ref[:, :1536]
    out_ref[...] = full_ref[:, 1536:]
    small = (own_ref[:8, 768:] + core_ref[:8, 768:]) + (hi_ref[:8, 768:] + both_ref[:8, 768:])
    small = jnp.concatenate([small, pltpu.roll(small, 64, 1)], axis=0)
    conv_ref[...] = small[:, :27]
    padded = jnp.concatenate([small, jnp.zeros((112, 128), F32)], axis=0)
    gain_ref[...] = jnp.transpose(padded)[27:28, :16]


def flip(tm_bits, clip_bits):
    pairs = [(t * 4 + k, (t ^ tm_bits) * 4 + (k ^ clip_bits)) for t in range(64) for k in range(4)]
    return lambda value: lax.ppermute(value, ("tm", "clip"), pairs)


def swap_all(value):
    return lax.all_to_all(value, "tm", 0, 0, tiled=True)


def body(frames, vis_pos, conv_weight, norm_gain, qkv_weight, out_weight, out_grad):
    ends = lax.axis_size("tm") - 1
    head = lax.ppermute(frames[:, 1:], "tm", [(i, i + 1) for i in range(ends)])
    tail = lax.ppermute(frames[:, :1], "tm", [(i + 1, i) for i in range(ends)])
    pos_row = vis_pos.reshape(1, VIS)
    gain = norm_gain.reshape(1, WIDTH)
    local, grad_rows = call(
        local_kernel,
        (shape((256, WIDTH), F32), shape((256, WIDTH), BF16)),
        streamed=3,
    )(frames, conv_weight, out_grad, pos_row)
    send, mixed = call(
        mix_kernel,
        (shape((64, 8, WIDTH), BF16), shape((256, WIDTH), F32)),
        [pltpu.VMEM((256, WIDTH), BF16)],
    )(local, grad_rows, head, tail, pos_row, conv_weight, gain)
    recv = swap_all(send)
    back, hidden, grad_tok, tok, attn = call(
        attend_kernel,
        (
            shape((64, 8, 768), BF16),
            shape((256, WIDTH), BF16),
            shape((256, WIDTH), BF16),
            shape((256, 3 * INNER), BF16),
            shape((256, INNER), BF16),
        ),
        [
            pltpu.VMEM((256, 3 * INNER), BF16),
            pltpu.VMEM((256, INNER), BF16),
            pltpu.VMEM((256, 3 * INNER), BF16),
        ],
        limit=16,
    )(recv, qkv_weight, out_weight)
    back_recv = swap_all(back)
    light = pl.CostEstimate(flops=1, bytes_accessed=1, transcendentals=0)
    terms = (hidden, tok, grad_tok, attn)
    give = call(part_kernel, shape((1024, 1024), BF16), cost=light)(*terms)
    got = flip(0, 1)(give)
    pieces = call(
        core_sum_kernel,
        (shape((1024, 128), BF16),) * 8,
        [pltpu.VMEM((1024, 1024), BF16)],
        cost=light,
    )(*terms, got)
    along_x = (flip(8, 0)(pieces[1]), flip(0, 2)(pieces[2]), flip(8, 2)(pieces[3]))
    along_y = [
        lax.ppermute(pieces[4 + k], "tm", [(i, (i + 16 * k) % 64) for i in range(64)]) for k in (1, 2, 3)
    ]
    block_out, small = call(
        finish_kernel,
        (shape(frames.shape, BF16), shape((64, 8, 128), BF16)),
        [
            pltpu.VMEM((256, 3 * INNER), BF16),
            pltpu.VMEM((256, WIDTH), F32),
            pltpu.VMEM((128, WIDTH), F32),
        ],
        streamed=6,
    )(out_weight, mixed, out_grad, frames, head, tail, pos_row, gain, back_recv)
    merged = call(merge_kernel, shape((64, 8, 512), BF16))(pieces[0], *along_x, pieces[4], *along_y)
    last_recv = swap_all(jnp.concatenate([merged, small], axis=2))
    own = call(tm_sum_kernel, shape((16, 896), F32))(last_recv)
    across = flip(0, 2)(own)
    grad_qkv, grad_out, grad_conv, grad_gain = call(
        last_kernel,
        (shape((16, 1536), F32), shape((16, 512), F32), shape((16, 27), F32), shape((1, 16), F32)),
        [pltpu.VMEM((16, 2048), F32)],
    )(own, flip(0, 1)(own), across, flip(0, 1)(across))
    return block_out, grad_qkv, grad_out.T, grad_conv.T, grad_gain.reshape(16)


def solution(mesh):
    return jax.shard_map(
        body,
        mesh=mesh,
        in_specs=(
            P("clip", "tm", None, None),
            P(),
            P(),
            P(),
            P(),
            P(),
            P("clip", "tm", None, None),
        ),
        out_specs=(
            P("clip", "tm", None, None),
            P("tm", None),
            P(None, "tm"),
            P(None, "tm"),
            P("tm"),
        ),
        check_vma=False,
    )
```

```python
import jax
import jax.numpy as jnp
from jax import lax
from jax.experimental import pallas as pl
from jax.experimental.pallas import tpu as pltpu
from jax.sharding import PartitionSpec as P

HEADS = 8
HDIM = 64
GRID = 28
EPSILON = 1e-05
SCORE_SCALE = 0.125
F32 = jnp.float32
BF16 = jnp.bfloat16

WIDTH = 1024
INNER = HEADS * HDIM
VIS = 64
CHUNK = 256
STEPS = [(a, b) for a in (-1, 0, 1) for b in (-1, 0, 1)]
SIDES = [s for s in range(9) if s != 4]


def call(kernel, out_shape, scratch=(), limit=12, streamed=0, cost=None):
    def run(*args):
        def streaming(*refs):
            sources, refs = refs[:streamed], refs[streamed:]
            plain = len(refs) - streamed - 1
            buffers, sems = refs[plain : plain + streamed], refs[-1]
            copies = [
                pltpu.make_async_copy(source, buffer, sems.at[n])
                for n, (source, buffer) in enumerate(zip(sources, buffers))
            ]
            for copy in copies:
                copy.start()
            kernel(lambda n: copies[n].wait(), *buffers, *refs[:plain])

        extra = [pltpu.VMEM(x.shape, x.dtype) for x in args[:streamed]]
        specs = [pl.BlockSpec(memory_space=pltpu.HBM)] * streamed
        specs += [pl.BlockSpec(memory_space=pltpu.VMEM)] * (len(args) - streamed)
        return pl.pallas_call(
            streaming if streamed else kernel,
            out_shape=out_shape,
            in_specs=specs,
            out_specs=jax.tree.map(home, out_shape),
            scratch_shapes=list(scratch)
            + (extra + [pltpu.SemaphoreType.DMA((streamed,))] if streamed else []),
            compiler_params=pltpu.CompilerParams(vmem_limit_bytes=limit * 1024 * 1024),
            cost_estimate=cost,
            name=kernel.__name__,
        )(*[pltpu.with_memory_space_constraint(x, pltpu.HBM) for x in args[:streamed]], *args[streamed:])

    return run


def home(out):
    return pl.BlockSpec(memory_space=pltpu.VMEM if isinstance(out, jax.ShapeDtypeStruct) else pltpu.HBM)


def shape(dims, dtype):
    return jax.ShapeDtypeStruct(dims, dtype)


def mm(left, right):
    return jnp.dot(left, right, preferred_element_type=F32)


def mm_nt(left, right):
    return lax.dot_general(left, right, (((1,), (1,)), ((), ())), preferred_element_type=F32)


def mm_tn(left, right):
    return lax.dot_general(left, right, (((0,), (0,)), ((), ())), preferred_element_type=F32)


def pack_matrix():
    row = lax.broadcasted_iota(jnp.int32, (256, 256), 0)
    col = lax.broadcasted_iota(jnp.int32, (256, 256), 1)
    return jnp.where(((row & 7) << 5) + (row >> 3) == col, 1.0, 0.0).astype(BF16)


def unpack_matrix():
    row = lax.broadcasted_iota(jnp.int32, (256, 256), 0)
    col = lax.broadcasted_iota(jnp.int32, (256, 256), 1)
    return jnp.where(((row & 31) << 3) + (row >> 5) == col, 1.0, 0.0).astype(BF16)


def tap_rows(pos_row):
    pos = pos_row[...]
    key = pos + 36 * ((pos * 2341) >> 16)
    across = jnp.broadcast_to(key.astype(F32), (VIS, VIS))
    diff = across - jnp.transpose(across)
    mats = [jnp.where(diff == 64 * STEPS[s][0] + STEPS[s][1], 1.0, 0.0) for s in SIDES]
    return jnp.concatenate(mats, axis=0).astype(BF16)


def norm_parts(mixed):
    average = jnp.mean(mixed, axis=-1, keepdims=True)
    centred = mixed - average
    variance = jnp.mean(centred * centred, axis=-1, keepdims=True)
    inv_std = lax.rsqrt(variance + EPSILON)
    return centred * inv_std, inv_std


def frame_at(frames_ref, head_ref, tail_ref, c, u, cols):
    if u == 0:
        return head_ref[c, 0, :, cols]
    if u == 3:
        return tail_ref[c, 0, :, cols]
    return frames_ref[c, u - 1, :, cols]


def moved_at(taps, cells):
    moved = mm(taps, cells)
    out = [moved[64 * k : 64 * k + 64] for k in range(8)]
    out.insert(4, cells.astype(F32))
    return out


def pack(source, out_ref):
    matrix = pack_matrix()
    for b in range(2):
        rows = [source(h, ct, b) for h in range(2) for ct in range(4)]
        moved = mm(matrix, jnp.concatenate(rows, axis=0))
        out_ref[32 * b : 32 * b + 32] = moved.reshape(32, 8, moved.shape[-1]).astype(BF16)


def unpack(in_ref, sink):
    matrix = unpack_matrix()
    for b in range(2):
        block = in_ref[32 * b : 32 * b + 32]
        moved = mm(matrix, block.reshape(256, block.shape[-1])).astype(BF16)
        for h in range(2):
            for ct in range(4):
                at = 32 * (4 * h + ct)
                sink(h, ct, b, moved[at : at + 32])


def unpack_to(in_ref, out_ref):
    width = in_ref.shape[-1]

    def sink(h, ct, b, block):
        at = 64 * ct + 32 * b
        out_ref[at : at + 32, width * h : width * h + width] = block

    unpack(in_ref, sink)


def unpack_two(in_ref, left_ref, right_ref):
    def sink(h, ct, b, block):
        at = 64 * ct + 32 * b
        (left_ref, right_ref)[h][at : at + 32, :] = block

    unpack(in_ref, sink)


def local_kernel(ready, frames_ref, w_ref, pos_row, mixed_ref):
    taps = tap_rows(pos_row)
    ready(0)
    ready(1)

    @pl.loop(0, WIDTH // CHUNK)
    def _(n):
        cols = pl.ds(pl.multiple_of(n * CHUNK, CHUNK), CHUNK)
        w = w_ref[:, cols]
        for c in range(2):
            acc = [frames_ref[c, t, :, cols].astype(F32) for t in range(2)]
            for u in (1, 2):
                moved = moved_at(taps, frames_ref[c, u - 1, :, cols])
                for s in range(9):
                    for t in range(2):
                        at = 9 * (u - t) + s
                        acc[t] = acc[t] + w[at : at + 1] * moved[s]
            for t in range(2):
                at = 64 * (2 * c + t)
                mixed_ref[at : at + 64, cols] = acc[t]


def mix_kernel(
    ready, grad_ref, part_ref, head_ref, tail_ref, pos_row, w_ref, gain_ref,
    send_ref, kept_ref, mixed_ref, hidden_ref, sem,
):
    taps = tap_rows(pos_row)

    @pl.loop(0, WIDTH // CHUNK)
    def _(n):
        cols = pl.ds(pl.multiple_of(n * CHUNK, CHUNK), CHUNK)
        w = w_ref[:, cols]
        for c in range(2):
            for t, halo_ref in enumerate((head_ref, tail_ref)):
                moved = moved_at(taps, halo_ref[c, 0, :, cols])
                rows = slice(64 * (2 * c + t), 64 * (2 * c + t) + 64)
                acc = part_ref[rows, cols]
                for s in range(9):
                    at = 18 * t + s
                    acc = acc + w[at : at + 1] * moved[s]
                mixed_ref[rows, cols] = acc

    keep = pltpu.make_async_copy(mixed_ref, kept_ref, sem)
    keep.start()
    for k in range(8):
        rows = slice(32 * k, 32 * k + 32)
        normed, _ = norm_parts(mixed_ref[rows])
        hidden_ref[rows] = (normed * gain_ref[...]).astype(BF16)

    def source(h, ct, b):
        if h == 0:
            return hidden_ref[64 * ct + 32 * b : 64 * ct + 32 * b + 32, :]
        return grad_ref[ct // 2, ct % 2, 32 * b : 32 * b + 32, :]

    ready(0)
    pack(source, send_ref)
    keep.wait()


def attend_kernel(
    recv_ref, wqkv_ref, wout_ref,
    send_ref, hidden_ref, grad_ref, tok_ref, attn_ref,
    qkv_ref, up_ref, back_ref,
):
    unpack_two(recv_ref, hidden_ref, grad_ref)
    up_ref[...] = mm_nt(grad_ref[...], wout_ref[...]).astype(BF16)
    for n in range(3):
        cols = slice(512 * n, 512 * n + 512)
        qkv_ref[:, cols] = mm(hidden_ref[...], wqkv_ref[:, cols]).astype(BF16)

    low = lax.broadcasted_iota(jnp.int32, (128, 128), 1) < 64

    def halves(value):
        zero = jnp.zeros_like(value)
        return jnp.where(low, value, zero), jnp.where(low, zero, value)

    for c in range(2):
        rows = slice(128 * c, 128 * c + 128)
        pairs = [slice(128 * p, 128 * p + 128) for p in range(4)]
        query = [qkv_ref[rows, 128 * p : 128 * p + 128] for p in range(4)]
        key = [qkv_ref[rows, INNER + 128 * p : INNER + 128 * p + 128] for p in range(4)]
        value = [qkv_ref[rows, 2 * INNER + 128 * p : 2 * INNER + 128 * p + 128] for p in range(4)]
        upstream = [up_ref[rows, at] for at in pairs]
        queries = [halves(x) for x in query]
        upstreams = [halves(x) for x in upstream]
        heads = [(p, e) for p in range(4) for e in range(2)]
        scores = [mm_nt(queries[p][e], key[p]) * SCORE_SCALE for p, e in heads]
        d_soft = [mm_nt(upstreams[p][e], value[p]).astype(BF16).astype(F32) for p, e in heads]
        scores = [jnp.exp(x - jnp.max(x, axis=-1, keepdims=True)) for x in scores]
        soft = [x / jnp.sum(x, axis=-1, keepdims=True) for x in scores]
        weights = [x.astype(BF16) for x in soft]
        inner = [jnp.sum(d * x, axis=-1, keepdims=True) for d, x in zip(d_soft, soft)]
        grads = [
            (x * (d - i) * SCORE_SCALE).astype(BF16) for d, x, i in zip(d_soft, soft, inner)
        ]
        for p in range(4):
            at = 128 * p
            both = slice(2 * p, 2 * p + 2)
            attn_ref[rows, at : at + 128] = mm(
                jnp.concatenate(weights[both], axis=1), jnp.concatenate(halves(value[p]), axis=0)
            ).astype(BF16)
            tok_ref[rows, at : at + 128] = mm(
                jnp.concatenate(grads[both], axis=1), jnp.concatenate(halves(key[p]), axis=0)
            ).astype(BF16)
            tok_ref[rows, INNER + at : INNER + at + 128] = mm_tn(
                jnp.concatenate(grads[both], axis=0), jnp.concatenate(queries[p], axis=0)
            ).astype(BF16)
            tok_ref[rows, 2 * INNER + at : 2 * INNER + at + 128] = mm_tn(
                jnp.concatenate(weights[both], axis=0), jnp.concatenate(upstreams[p], axis=0)
            ).astype(BF16)

    for n in range(2):
        cols = slice(512 * n, 512 * n + 512)
        back_ref[:, cols] = mm_nt(tok_ref[...], wqkv_ref[cols, :]).astype(BF16)
    back_ref[:, WIDTH:] = attn_ref[...]

    def source(h, ct, b):
        at = 64 * ct + 32 * b
        return back_ref[at : at + 32, 768 * h : 768 * h + 768]

    pack(source, send_ref)


def places():
    tm, clip = lax.axis_index("tm"), lax.axis_index("clip")
    return lax.rem(lax.div(tm, 8), 2), lax.div(tm, 16), lax.div(clip, 2), lax.rem(clip, 2)


def weight_half(hidden_ref, tok_ref, grad_ref, attn_ref, half, sink):
    @pl.when(half == 0)
    def _():
        for n in range(4):
            sink(256 * n, mm_tn(hidden_ref[...], tok_ref[:, 256 * n : 256 * n + 256]))

    @pl.when(half == 1)
    def _():
        for n in range(2):
            sink(256 * n, mm_tn(hidden_ref[...], tok_ref[:, 1024 + 256 * n : 1280 + 256 * n]))
        for n in range(2):
            sink(512 + 256 * n, mm_tn(grad_ref[...], attn_ref[:, 256 * n : 256 * n + 256]))


def part_kernel(hidden_ref, tok_ref, grad_ref, attn_ref, give_ref):
    core = places()[3]

    def sink(at, value):
        give_ref[:, at : at + 256] = value.astype(BF16)

    weight_half(hidden_ref, tok_ref, grad_ref, attn_ref, 1 - core, sink)


def core_sum_kernel(hidden_ref, tok_ref, grad_ref, attn_ref, got_ref, *refs):
    piece_refs, both_ref = refs[:8], refs[8]
    x_lo, y, x_hi, core = places()

    def sink(at, value):
        both = value + got_ref[:, at : at + 256].astype(F32)
        both_ref[:, at : at + 256] = both.astype(BF16)

    weight_half(hidden_ref, tok_ref, grad_ref, attn_ref, core, sink)

    def part(at):
        return both_ref[:, pl.ds(pl.multiple_of(at, 128), 128)]

    for piece, (flip_lo, flip_hi) in enumerate(((0, 0), (1, 0), (0, 1), (1, 1))):
        lo = x_lo if flip_lo == 0 else 1 - x_lo
        hi = x_hi if flip_hi == 0 else 1 - x_hi
        piece_refs[piece][...] = part(256 * hi + 128 * lo)
    for k in range(4):
        piece_refs[4 + k][...] = part(512 + 128 * ((y + k) & 3))


def merge_kernel(*refs):
    out_ref = refs[-1]
    for side in range(2):
        a, b, c, d = (ref[...].astype(F32) for ref in refs[4 * side : 4 * side + 4])
        total = ((a + b) + (c + d)).reshape(64, 16, 128)
        for half in range(2):
            at = 256 * side + 128 * half
            out_ref[:, :, at : at + 128] = total[:, 8 * half : 8 * half + 8].astype(BF16)


def finish_kernel(
    ready, wout_ref, mixed_ref, grad_ref, frames_ref, head_ref, tail_ref, pos_row, gain_ref, recv_ref,
    out_ref, small_ref,
    back_ref, gm_ref, rows_ref,
):
    unpack_to(recv_ref, back_ref)
    gain = gain_ref[...]
    rows_ref[...] = jnp.zeros_like(rows_ref)
    for n in range(6):
        ready(n)
    for ct in range(4):
        at = slice(64 * ct, 64 * ct + 64)
        proj = mm(back_ref[at, WIDTH:], wout_ref[...])
        out_ref[ct // 2, ct % 2] = (mixed_ref[at] + proj).astype(BF16)
    gain_sum = jnp.zeros((8, WIDTH), F32)
    for k in range(8):
        rows = slice(32 * k, 32 * k + 32)
        normed, inv_std = norm_parts(mixed_ref[rows])
        grad_hidden = back_ref[rows, :WIDTH].astype(F32)
        prod = grad_hidden * normed
        gain_sum = gain_sum + jnp.sum(prod.reshape(4, 8, WIDTH), axis=0)
        scaled = grad_hidden * gain
        first = jnp.mean(scaled, axis=-1, keepdims=True)
        second = jnp.mean(prod * gain, axis=-1, keepdims=True)
        ct, half = k // 2, k % 2
        upstream = grad_ref[ct // 2, ct % 2, 32 * half : 32 * half + 32, :].astype(F32)
        gm_ref[rows] = inv_std * (scaled - first - normed * second) + upstream
    rows_ref[27:28, :] = jnp.sum(gain_sum, axis=0, keepdims=True)
    taps = tap_rows(pos_row)

    @pl.loop(0, WIDTH // CHUNK)
    def _(n):
        cols = pl.ds(pl.multiple_of(n * CHUNK, CHUNK), CHUNK)
        acc = [jnp.zeros((8, CHUNK), F32) for _ in range(27)]
        for c in range(2):
            gm = [gm_ref[64 * (2 * c + t) : 64 * (2 * c + t) + 64, cols] for t in range(2)]
            for u in range(4):
                moved = moved_at(taps, frame_at(frames_ref, head_ref, tail_ref, c, u, cols))
                for s in range(9):
                    for t in range(2):
                        lag = u - t
                        if 0 <= lag <= 2:
                            prod = (gm[t] * moved[s]).reshape(8, 8, CHUNK)
                            acc[9 * lag + s] = acc[9 * lag + s] + jnp.sum(prod, axis=0)
        for at in range(27):
            rows_ref[at : at + 1, cols] = jnp.sum(acc[at], axis=0, keepdims=True)

    rows_ref[64:96, :] = rows_ref[0:32, :]
    turned = jnp.transpose(rows_ref[...]).reshape(64, 16, 128)
    left = lax.broadcasted_iota(jnp.int32, (64, 8, 128), 2) < 64
    small_ref[...] = jnp.where(left, turned[:, :8], turned[:, 8:]).astype(BF16)


def tm_sum_kernel(recv_ref, out_ref):
    def over(first, last, at):
        total = recv_ref[first, :, at : at + 128].astype(F32)
        for src in range(first + 1, last):
            total = total + recv_ref[src, :, at : at + 128].astype(F32)
        return total

    for half in range(2):
        rows = slice(8 * half, 8 * half + 8)
        kept = [[over(16 * y + 8 * lo, 16 * y + 8 * lo + 8, 128 * half) for lo in range(2)] for y in range(4)]
        for lo in range(2):
            out_ref[rows, 128 * lo : 128 * lo + 128] = (kept[0][lo] + kept[1][lo]) + (kept[2][lo] + kept[3][lo])
        for y in range(4):
            at = 256 + 128 * y
            out_ref[rows, at : at + 128] = over(16 * y, 16 * y + 16, 256 + 128 * half)
    out_ref[:8, 768:] = over(0, 64, 512)
    out_ref[8:, 768:] = jnp.zeros((8, 128), F32)


def last_kernel(own_ref, core_ref, hi_ref, both_ref, qkv_ref, out_ref, conv_ref, gain_ref, full_ref):
    _, _, x_hi, core = places()
    mine = pl.multiple_of(1024 * core, 1024)
    other = pl.multiple_of(1024 - 1024 * core, 1024)
    here = pl.multiple_of(256 * x_hi, 256)
    there = pl.multiple_of(256 - 256 * x_hi, 256)
    full_ref[:, pl.ds(mine + here, 256)] = own_ref[:, :256]
    full_ref[:, pl.ds(mine + there, 256)] = hi_ref[:, :256]
    full_ref[:, pl.ds(other + here, 256)] = core_ref[:, :256]
    full_ref[:, pl.ds(other + there, 256)] = both_ref[:, :256]
    full_ref[:, pl.ds(mine + 512, 512)] = own_ref[:, 256:768] + hi_ref[:, 256:768]
    full_ref[:, pl.ds(other + 512, 512)] = core_ref[:, 256:768] + both_ref[:, 256:768]
    qkv_ref[...] = full_ref[:, :1536]
    out_ref[...] = full_ref[:, 1536:]
    small = (own_ref[:8, 768:] + core_ref[:8, 768:]) + (hi_ref[:8, 768:] + both_ref[:8, 768:])
    small = jnp.concatenate([small, pltpu.roll(small, 64, 1)], axis=0)
    conv_ref[...] = small[:, :27]
    padded = jnp.concatenate([small, jnp.zeros((112, 128), F32)], axis=0)
    gain_ref[...] = jnp.transpose(padded)[27:28, :16]


def flip(tm_bits, clip_bits):
    pairs = [(t * 4 + k, (t ^ tm_bits) * 4 + (k ^ clip_bits)) for t in range(64) for k in range(4)]
    return lambda value: lax.ppermute(value, ("tm", "clip"), pairs)


def swap_all(value):
    return lax.all_to_all(value, "tm", 0, 0, tiled=True)


def body(frames, vis_pos, conv_weight, norm_gain, qkv_weight, out_weight, out_grad):
    ends = lax.axis_size("tm") - 1
    head = lax.ppermute(frames[:, 1:], "tm", [(i, i + 1) for i in range(ends)])
    tail = lax.ppermute(frames[:, :1], "tm", [(i + 1, i) for i in range(ends)])
    pos_row = vis_pos.reshape(1, VIS)
    gain = norm_gain.reshape(1, WIDTH)
    local = call(local_kernel, shape((256, WIDTH), F32), streamed=2)(frames, conv_weight, pos_row)
    send, mixed = call(
        mix_kernel,
        (shape((64, 8, WIDTH), BF16), pltpu.HBM((256, WIDTH), F32)),
        [pltpu.VMEM((256, WIDTH), F32), pltpu.VMEM((256, WIDTH), BF16), pltpu.SemaphoreType.DMA],
        streamed=1,
    )(out_grad, local, head, tail, pos_row, conv_weight, gain)
    recv = swap_all(send)
    back, hidden, grad_tok, tok, attn = call(
        attend_kernel,
        (
            shape((64, 8, 768), BF16),
            shape((256, WIDTH), BF16),
            shape((256, WIDTH), BF16),
            shape((256, 3 * INNER), BF16),
            shape((256, INNER), BF16),
        ),
        [
            pltpu.VMEM((256, 3 * INNER), BF16),
            pltpu.VMEM((256, INNER), BF16),
            pltpu.VMEM((256, 3 * INNER), BF16),
        ],
        limit=16,
    )(recv, qkv_weight, out_weight)
    back_recv = swap_all(back)
    light = pl.CostEstimate(flops=1, bytes_accessed=1, transcendentals=0)
    terms = (hidden, tok, grad_tok, attn)
    give = call(part_kernel, shape((1024, 1024), BF16), cost=light)(*terms)
    got = flip(0, 1)(give)
    pieces = call(
        core_sum_kernel,
        (shape((1024, 128), BF16),) * 8,
        [pltpu.VMEM((1024, 1024), BF16)],
        cost=light,
    )(*terms, got)
    along_x = (flip(8, 0)(pieces[1]), flip(0, 2)(pieces[2]), flip(8, 2)(pieces[3]))
    along_y = [
        lax.ppermute(pieces[4 + k], "tm", [(i, (i + 16 * k) % 64) for i in range(64)]) for k in (1, 2, 3)
    ]
    block_out, small = call(
        finish_kernel,
        (shape(frames.shape, BF16), shape((64, 8, 128), BF16)),
        [
            pltpu.VMEM((256, 3 * INNER), BF16),
            pltpu.VMEM((256, WIDTH), F32),
            pltpu.VMEM((128, WIDTH), F32),
        ],
        streamed=6,
    )(out_weight, mixed, out_grad, frames, head, tail, pos_row, gain, back_recv)
    merged = call(merge_kernel, shape((64, 8, 512), BF16))(pieces[0], *along_x, pieces[4], *along_y)
    last_recv = swap_all(jnp.concatenate([merged, small], axis=2))
    own = call(tm_sum_kernel, shape((16, 896), F32))(last_recv)
    across = flip(0, 2)(own)
    grad_qkv, grad_out, grad_conv, grad_gain = call(
        last_kernel,
        (shape((16, 1536), F32), shape((16, 512), F32), shape((16, 27), F32), shape((1, 16), F32)),
        [pltpu.VMEM((16, 2048), F32)],
    )(own, flip(0, 1)(own), across, flip(0, 1)(across))
    return block_out, grad_qkv, grad_out.T, grad_conv.T, grad_gain.reshape(16)


def solution(mesh):
    return jax.shard_map(
        body,
        mesh=mesh,
        in_specs=(
            P("clip", "tm", None, None),
            P(),
            P(),
            P(),
            P(),
            P(),
            P("clip", "tm", None, None),
        ),
        out_specs=(
            P("clip", "tm", None, None),
            P("tm", None),
            P(None, "tm"),
            P(None, "tm"),
            P("tm"),
        ),
        check_vma=False,
    )
```

```python
import jax
import jax.numpy as jnp
from jax import lax
from jax.experimental import pallas as pl
from jax.experimental.pallas import tpu as pltpu
from jax.sharding import PartitionSpec as P

HEADS = 8
HDIM = 64
GRID = 28
EPSILON = 1e-05
SCORE_SCALE = 0.125
F32 = jnp.float32
BF16 = jnp.bfloat16

WIDTH = 1024
INNER = HEADS * HDIM
VIS = 64
CHUNK = 256
STEPS = [(a, b) for a in (-1, 0, 1) for b in (-1, 0, 1)]
SIDES = [s for s in range(9) if s != 4]


def call(kernel, out_shape, scratch=(), limit=12, streamed=0, cost=None):
    def run(*args):
        def streaming(*refs):
            sources, refs = refs[:streamed], refs[streamed:]
            plain = len(refs) - streamed - 1
            buffers, sems = refs[plain : plain + streamed], refs[-1]
            copies = [
                pltpu.make_async_copy(source, buffer, sems.at[n])
                for n, (source, buffer) in enumerate(zip(sources, buffers))
            ]
            for copy in copies:
                copy.start()
            kernel(lambda n: copies[n].wait(), *buffers, *refs[:plain])

        extra = [pltpu.VMEM(x.shape, x.dtype) for x in args[:streamed]]
        specs = [pl.BlockSpec(memory_space=pltpu.HBM)] * streamed
        specs += [pl.BlockSpec(memory_space=pltpu.VMEM)] * (len(args) - streamed)
        return pl.pallas_call(
            streaming if streamed else kernel,
            out_shape=out_shape,
            in_specs=specs,
            out_specs=jax.tree.map(home, out_shape),
            scratch_shapes=list(scratch)
            + (extra + [pltpu.SemaphoreType.DMA((streamed,))] if streamed else []),
            compiler_params=pltpu.CompilerParams(vmem_limit_bytes=limit * 1024 * 1024),
            cost_estimate=cost,
            name=kernel.__name__,
        )(*[pltpu.with_memory_space_constraint(x, pltpu.HBM) for x in args[:streamed]], *args[streamed:])

    return run


def home(out):
    return pl.BlockSpec(memory_space=pltpu.VMEM if isinstance(out, jax.ShapeDtypeStruct) else pltpu.HBM)


def shape(dims, dtype):
    return jax.ShapeDtypeStruct(dims, dtype)


def mm(left, right):
    return jnp.dot(left, right, preferred_element_type=F32)


def mm_nt(left, right):
    return lax.dot_general(left, right, (((1,), (1,)), ((), ())), preferred_element_type=F32)


def mm_tn(left, right):
    return lax.dot_general(left, right, (((0,), (0,)), ((), ())), preferred_element_type=F32)


def pack_matrix():
    row = lax.broadcasted_iota(jnp.int32, (256, 256), 0)
    col = lax.broadcasted_iota(jnp.int32, (256, 256), 1)
    return jnp.where(((row & 7) << 5) + (row >> 3) == col, 1.0, 0.0).astype(BF16)


def unpack_matrix():
    row = lax.broadcasted_iota(jnp.int32, (256, 256), 0)
    col = lax.broadcasted_iota(jnp.int32, (256, 256), 1)
    return jnp.where(((row & 31) << 3) + (row >> 5) == col, 1.0, 0.0).astype(BF16)


def tap_rows(pos_row):
    pos = pos_row[...]
    key = pos + 36 * ((pos * 2341) >> 16)
    across = jnp.broadcast_to(key.astype(F32), (VIS, VIS))
    diff = across - jnp.transpose(across)
    mats = [jnp.where(diff == 64 * STEPS[s][0] + STEPS[s][1], 1.0, 0.0) for s in SIDES]
    return jnp.concatenate(mats, axis=0).astype(BF16)


def norm_parts(mixed):
    average = jnp.mean(mixed, axis=-1, keepdims=True)
    centred = mixed - average
    variance = jnp.mean(centred * centred, axis=-1, keepdims=True)
    inv_std = lax.rsqrt(variance + EPSILON)
    return centred * inv_std, inv_std


def frame_at(frames_ref, head_ref, tail_ref, c, u, cols):
    if u == 0:
        return head_ref[c, 0, :, cols]
    if u == 3:
        return tail_ref[c, 0, :, cols]
    return frames_ref[c, u - 1, :, cols]


def moved_at(taps, cells):
    moved = mm(taps, cells)
    out = [moved[64 * k : 64 * k + 64] for k in range(8)]
    out.insert(4, cells.astype(F32))
    return out


def pack(source, out_ref):
    matrix = pack_matrix()
    for b in range(2):
        rows = [source(h, ct, b) for h in range(2) for ct in range(4)]
        moved = mm(matrix, jnp.concatenate(rows, axis=0))
        out_ref[32 * b : 32 * b + 32] = moved.reshape(32, 8, moved.shape[-1]).astype(BF16)


def unpack(in_ref, sink):
    matrix = unpack_matrix()
    for b in range(2):
        block = in_ref[32 * b : 32 * b + 32]
        moved = mm(matrix, block.reshape(256, block.shape[-1])).astype(BF16)
        for h in range(2):
            for ct in range(4):
                at = 32 * (4 * h + ct)
                sink(h, ct, b, moved[at : at + 32])


def unpack_to(in_ref, out_ref):
    width = in_ref.shape[-1]

    def sink(h, ct, b, block):
        at = 64 * ct + 32 * b
        out_ref[at : at + 32, width * h : width * h + width] = block

    unpack(in_ref, sink)


def unpack_two(in_ref, left_ref, right_ref):
    def sink(h, ct, b, block):
        at = 64 * ct + 32 * b
        (left_ref, right_ref)[h][at : at + 32, :] = block

    unpack(in_ref, sink)


def local_kernel(ready, frames_ref, w_ref, pos_row, mixed_ref):
    taps = tap_rows(pos_row)
    ready(0)
    ready(1)

    @pl.loop(0, WIDTH // CHUNK)
    def _(n):
        cols = pl.ds(pl.multiple_of(n * CHUNK, CHUNK), CHUNK)
        w = w_ref[:, cols]
        for c in range(2):
            acc = [frames_ref[c, t, :, cols].astype(F32) for t in range(2)]
            for u in (1, 2):
                moved = moved_at(taps, frames_ref[c, u - 1, :, cols])
                for s in range(9):
                    for t in range(2):
                        at = 9 * (u - t) + s
                        acc[t] = acc[t] + w[at : at + 1] * moved[s]
            for t in range(2):
                at = 64 * (2 * c + t)
                mixed_ref[at : at + 64, cols] = acc[t]


def mix_kernel(
    ready, grad_ref, part_ref, head_ref, tail_ref, pos_row, w_ref, gain_ref,
    send_ref, kept_ref, mixed_ref, hidden_ref, sem,
):
    taps = tap_rows(pos_row)

    @pl.loop(0, WIDTH // CHUNK)
    def _(n):
        cols = pl.ds(pl.multiple_of(n * CHUNK, CHUNK), CHUNK)
        w = w_ref[:, cols]
        for c in range(2):
            for t, halo_ref in enumerate((head_ref, tail_ref)):
                moved = moved_at(taps, halo_ref[c, 0, :, cols])
                rows = slice(64 * (2 * c + t), 64 * (2 * c + t) + 64)
                acc = part_ref[rows, cols]
                for s in range(9):
                    at = 18 * t + s
                    acc = acc + w[at : at + 1] * moved[s]
                mixed_ref[rows, cols] = acc

    keep = pltpu.make_async_copy(mixed_ref, kept_ref, sem)
    keep.start()
    for k in range(8):
        rows = slice(32 * k, 32 * k + 32)
        normed, _ = norm_parts(mixed_ref[rows])
        hidden_ref[rows] = (normed * gain_ref[...]).astype(BF16)

    def source(h, ct, b):
        if h == 0:
            return hidden_ref[64 * ct + 32 * b : 64 * ct + 32 * b + 32, :]
        return grad_ref[ct // 2, ct % 2, 32 * b : 32 * b + 32, :]

    ready(0)
    pack(source, send_ref)
    keep.wait()


def places():
    tm, clip = lax.axis_index("tm"), lax.axis_index("clip")
    return lax.rem(lax.div(tm, 8), 2), lax.div(tm, 16), lax.div(clip, 2), lax.rem(clip, 2)


def weight_half(hidden_ref, tok_ref, grad_ref, attn_ref, half, sink):
    @pl.when(half == 0)
    def _():
        for n in range(4):
            sink(256 * n, mm_tn(hidden_ref[...], tok_ref[:, 256 * n : 256 * n + 256]))

    @pl.when(half == 1)
    def _():
        for n in range(2):
            sink(256 * n, mm_tn(hidden_ref[...], tok_ref[:, 1024 + 256 * n : 1280 + 256 * n]))
        for n in range(2):
            sink(512 + 256 * n, mm_tn(grad_ref[...], attn_ref[:, 256 * n : 256 * n + 256]))


def attend_kernel(
    recv_ref, wqkv_ref, wout_ref,
    send_ref, give_ref, *refs,
):
    hidden_ref, grad_ref, tok_ref, attn_ref = refs[4:8]
    qkv_ref, up_ref, back_ref, half_ref, sems = refs[8:]
    copies = [pltpu.make_async_copy(refs[4 + n], refs[n], sems.at[n]) for n in range(4)]
    copies.append(pltpu.make_async_copy(half_ref, give_ref, sems.at[4]))
    unpack_two(recv_ref, hidden_ref, grad_ref)
    up_ref[...] = mm_nt(grad_ref[...], wout_ref[...]).astype(BF16)
    for n in range(3):
        cols = slice(512 * n, 512 * n + 512)
        qkv_ref[:, cols] = mm(hidden_ref[...], wqkv_ref[:, cols]).astype(BF16)

    low = lax.broadcasted_iota(jnp.int32, (128, 128), 1) < 64

    def halves(value):
        zero = jnp.zeros_like(value)
        return jnp.where(low, value, zero), jnp.where(low, zero, value)

    for c in range(2):
        rows = slice(128 * c, 128 * c + 128)
        pairs = [slice(128 * p, 128 * p + 128) for p in range(4)]
        query = [qkv_ref[rows, 128 * p : 128 * p + 128] for p in range(4)]
        key = [qkv_ref[rows, INNER + 128 * p : INNER + 128 * p + 128] for p in range(4)]
        value = [qkv_ref[rows, 2 * INNER + 128 * p : 2 * INNER + 128 * p + 128] for p in range(4)]
        upstream = [up_ref[rows, at] for at in pairs]
        queries = [halves(x) for x in query]
        upstreams = [halves(x) for x in upstream]
        heads = [(p, e) for p in range(4) for e in range(2)]
        scores = [mm_nt(queries[p][e], key[p]) * SCORE_SCALE for p, e in heads]
        d_soft = [mm_nt(upstreams[p][e], value[p]).astype(BF16).astype(F32) for p, e in heads]
        scores = [jnp.exp(x - jnp.max(x, axis=-1, keepdims=True)) for x in scores]
        soft = [x / jnp.sum(x, axis=-1, keepdims=True) for x in scores]
        weights = [x.astype(BF16) for x in soft]
        inner = [jnp.sum(d * x, axis=-1, keepdims=True) for d, x in zip(d_soft, soft)]
        grads = [
            (x * (d - i) * SCORE_SCALE).astype(BF16) for d, x, i in zip(d_soft, soft, inner)
        ]
        for p in range(4):
            at = 128 * p
            both = slice(2 * p, 2 * p + 2)
            attn_ref[rows, at : at + 128] = mm(
                jnp.concatenate(weights[both], axis=1), jnp.concatenate(halves(value[p]), axis=0)
            ).astype(BF16)
            tok_ref[rows, at : at + 128] = mm(
                jnp.concatenate(grads[both], axis=1), jnp.concatenate(halves(key[p]), axis=0)
            ).astype(BF16)
            tok_ref[rows, INNER + at : INNER + at + 128] = mm_tn(
                jnp.concatenate(grads[both], axis=0), jnp.concatenate(queries[p], axis=0)
            ).astype(BF16)
            tok_ref[rows, 2 * INNER + at : 2 * INNER + at + 128] = mm_tn(
                jnp.concatenate(weights[both], axis=0), jnp.concatenate(upstreams[p], axis=0)
            ).astype(BF16)

    def keep(at, value):
        half_ref[:, at : at + 256] = value.astype(BF16)

    weight_half(hidden_ref, tok_ref, grad_ref, attn_ref, 1 - places()[3], keep)
    for copy in copies:
        copy.start()
    for n in range(2):
        cols = slice(512 * n, 512 * n + 512)
        back_ref[:, cols] = mm_nt(tok_ref[...], wqkv_ref[cols, :]).astype(BF16)
    back_ref[:, WIDTH:] = attn_ref[...]

    def source(h, ct, b):
        at = 64 * ct + 32 * b
        return back_ref[at : at + 32, 768 * h : 768 * h + 768]

    pack(source, send_ref)
    for copy in copies:
        copy.wait()


def core_sum_kernel(ready, hidden_ref, grad_ref, tok_ref, attn_ref, got_ref, *refs):
    piece_refs, both_ref = refs[:8], refs[8]
    x_lo, y, x_hi, core = places()

    for n in range(4):
        ready(n)

    def sink(at, value):
        both = value + got_ref[:, at : at + 256].astype(F32)
        both_ref[:, at : at + 256] = both.astype(BF16)

    weight_half(hidden_ref, tok_ref, grad_ref, attn_ref, core, sink)

    def part(at):
        return both_ref[:, pl.ds(pl.multiple_of(at, 128), 128)]

    for piece, (flip_lo, flip_hi) in enumerate(((0, 0), (1, 0), (0, 1), (1, 1))):
        lo = x_lo if flip_lo == 0 else 1 - x_lo
        hi = x_hi if flip_hi == 0 else 1 - x_hi
        piece_refs[piece][...] = part(256 * hi + 128 * lo)
    for k in range(4):
        piece_refs[4 + k][...] = part(512 + 128 * ((y + k) & 3))


def merge_kernel(*refs):
    out_ref = refs[-1]
    for side in range(2):
        a, b, c, d = (ref[...].astype(F32) for ref in refs[4 * side : 4 * side + 4])
        total = ((a + b) + (c + d)).reshape(64, 16, 128)
        for half in range(2):
            at = 256 * side + 128 * half
            out_ref[:, :, at : at + 128] = total[:, 8 * half : 8 * half + 8].astype(BF16)


def finish_kernel(
    ready, wout_ref, mixed_ref, grad_ref, frames_ref, head_ref, tail_ref, pos_row, gain_ref, recv_ref,
    out_ref, small_ref,
    back_ref, gm_ref, rows_ref, block_ref, sem,
):
    unpack_to(recv_ref, back_ref)
    gain = gain_ref[...]
    rows_ref[...] = jnp.zeros_like(rows_ref)
    ready(0)
    ready(1)
    for ct in range(4):
        at = slice(64 * ct, 64 * ct + 64)
        proj = mm(back_ref[at, WIDTH:], wout_ref[...])
        block_ref[ct // 2, ct % 2] = (mixed_ref[at] + proj).astype(BF16)
    write = pltpu.make_async_copy(block_ref, out_ref, sem)
    write.start()
    ready(2)
    gain_sum = jnp.zeros((8, WIDTH), F32)
    for k in range(8):
        rows = slice(32 * k, 32 * k + 32)
        normed, inv_std = norm_parts(mixed_ref[rows])
        grad_hidden = back_ref[rows, :WIDTH].astype(F32)
        prod = grad_hidden * normed
        gain_sum = gain_sum + jnp.sum(prod.reshape(4, 8, WIDTH), axis=0)
        scaled = grad_hidden * gain
        first = jnp.mean(scaled, axis=-1, keepdims=True)
        second = jnp.mean(prod * gain, axis=-1, keepdims=True)
        ct, half = k // 2, k % 2
        upstream = grad_ref[ct // 2, ct % 2, 32 * half : 32 * half + 32, :].astype(F32)
        gm_ref[rows] = inv_std * (scaled - first - normed * second) + upstream
    rows_ref[27:28, :] = jnp.sum(gain_sum, axis=0, keepdims=True)
    taps = tap_rows(pos_row)
    for n in (3, 4, 5):
        ready(n)

    @pl.loop(0, WIDTH // CHUNK)
    def _(n):
        cols = pl.ds(pl.multiple_of(n * CHUNK, CHUNK), CHUNK)
        acc = [jnp.zeros((8, CHUNK), F32) for _ in range(27)]
        for c in range(2):
            gm = [gm_ref[64 * (2 * c + t) : 64 * (2 * c + t) + 64, cols] for t in range(2)]
            for u in range(4):
                moved = moved_at(taps, frame_at(frames_ref, head_ref, tail_ref, c, u, cols))
                for s in range(9):
                    for t in range(2):
                        lag = u - t
                        if 0 <= lag <= 2:
                            prod = (gm[t] * moved[s]).reshape(8, 8, CHUNK)
                            acc[9 * lag + s] = acc[9 * lag + s] + jnp.sum(prod, axis=0)
        for at in range(27):
            rows_ref[at : at + 1, cols] = jnp.sum(acc[at], axis=0, keepdims=True)

    rows_ref[64:96, :] = rows_ref[0:32, :]
    turned = jnp.transpose(rows_ref[...]).reshape(64, 16, 128)
    left = lax.broadcasted_iota(jnp.int32, (64, 8, 128), 2) < 64
    small_ref[...] = jnp.where(left, turned[:, :8], turned[:, 8:]).astype(BF16)
    write.wait()


def tm_sum_kernel(recv_ref, out_ref):
    def over(first, last, at):
        total = recv_ref[first, :, at : at + 128].astype(F32)
        for src in range(first + 1, last):
            total = total + recv_ref[src, :, at : at + 128].astype(F32)
        return total

    for half in range(2):
        rows = slice(8 * half, 8 * half + 8)
        kept = [[over(16 * y + 8 * lo, 16 * y + 8 * lo + 8, 128 * half) for lo in range(2)] for y in range(4)]
        for lo in range(2):
            out_ref[rows, 128 * lo : 128 * lo + 128] = (kept[0][lo] + kept[1][lo]) + (kept[2][lo] + kept[3][lo])
        for y in range(4):
            at = 256 + 128 * y
            out_ref[rows, at : at + 128] = over(16 * y, 16 * y + 16, 256 + 128 * half)
    out_ref[:8, 768:] = over(0, 64, 512)
    out_ref[8:, 768:] = jnp.zeros((8, 128), F32)


def last_kernel(own_ref, core_ref, hi_ref, both_ref, qkv_ref, out_ref, conv_ref, gain_ref, full_ref):
    _, _, x_hi, core = places()
    mine = pl.multiple_of(1024 * core, 1024)
    other = pl.multiple_of(1024 - 1024 * core, 1024)
    here = pl.multiple_of(256 * x_hi, 256)
    there = pl.multiple_of(256 - 256 * x_hi, 256)
    full_ref[:, pl.ds(mine + here, 256)] = own_ref[:, :256]
    full_ref[:, pl.ds(mine + there, 256)] = hi_ref[:, :256]
    full_ref[:, pl.ds(other + here, 256)] = core_ref[:, :256]
    full_ref[:, pl.ds(other + there, 256)] = both_ref[:, :256]
    full_ref[:, pl.ds(mine + 512, 512)] = own_ref[:, 256:768] + hi_ref[:, 256:768]
    full_ref[:, pl.ds(other + 512, 512)] = core_ref[:, 256:768] + both_ref[:, 256:768]
    qkv_ref[...] = full_ref[:, :1536]
    out_ref[...] = full_ref[:, 1536:]
    small = (own_ref[:8, 768:] + core_ref[:8, 768:]) + (hi_ref[:8, 768:] + both_ref[:8, 768:])
    small = jnp.concatenate([small, pltpu.roll(small, 64, 1)], axis=0)
    conv_ref[...] = small[:, :27]
    padded = jnp.concatenate([small, jnp.zeros((112, 128), F32)], axis=0)
    gain_ref[...] = jnp.transpose(padded)[27:28, :16]


def flip(tm_bits, clip_bits):
    pairs = [(t * 4 + k, (t ^ tm_bits) * 4 + (k ^ clip_bits)) for t in range(64) for k in range(4)]
    return lambda value: lax.ppermute(value, ("tm", "clip"), pairs)


def swap_all(value):
    return lax.all_to_all(value, "tm", 0, 0, tiled=True)


def body(frames, vis_pos, conv_weight, norm_gain, qkv_weight, out_weight, out_grad):
    ends = lax.axis_size("tm") - 1
    head = lax.ppermute(frames[:, 1:], "tm", [(i, i + 1) for i in range(ends)])
    tail = lax.ppermute(frames[:, :1], "tm", [(i + 1, i) for i in range(ends)])
    pos_row = vis_pos.reshape(1, VIS)
    gain = norm_gain.reshape(1, WIDTH)
    local = call(local_kernel, shape((256, WIDTH), F32), streamed=2)(frames, conv_weight, pos_row)
    send, mixed = call(
        mix_kernel,
        (shape((64, 8, WIDTH), BF16), pltpu.HBM((256, WIDTH), F32)),
        [pltpu.VMEM((256, WIDTH), F32), pltpu.VMEM((256, WIDTH), BF16), pltpu.SemaphoreType.DMA],
        streamed=1,
    )(out_grad, local, head, tail, pos_row, conv_weight, gain)
    recv = swap_all(send)
    kept = ((256, WIDTH), (256, WIDTH), (256, 3 * INNER), (256, INNER))
    back, give, *terms = call(
        attend_kernel,
        (
            shape((64, 8, 768), BF16),
            pltpu.HBM((1024, 1024), BF16),
            *(pltpu.HBM(dims, BF16) for dims in kept),
        ),
        [
            *(pltpu.VMEM(dims, BF16) for dims in kept),
            pltpu.VMEM((256, 3 * INNER), BF16),
            pltpu.VMEM((256, INNER), BF16),
            pltpu.VMEM((256, 3 * INNER), BF16),
            pltpu.VMEM((1024, 1024), BF16),
            pltpu.SemaphoreType.DMA((5,)),
        ],
        limit=18,
    )(recv, qkv_weight, out_weight)
    back_recv = swap_all(back)
    light = pl.CostEstimate(flops=1, bytes_accessed=1, transcendentals=0)
    got = flip(0, 1)(give)
    pieces = call(
        core_sum_kernel,
        (shape((1024, 128), BF16),) * 8,
        [pltpu.VMEM((1024, 1024), BF16)],
        streamed=4,
        cost=light,
    )(*terms, got)
    along_x = (flip(8, 0)(pieces[1]), flip(0, 2)(pieces[2]), flip(8, 2)(pieces[3]))
    along_y = [
        lax.ppermute(pieces[4 + k], "tm", [(i, (i + 16 * k) % 64) for i in range(64)]) for k in (1, 2, 3)
    ]
    block_out, small = call(
        finish_kernel,
        (pltpu.HBM(frames.shape, BF16), shape((64, 8, 128), BF16)),
        [
            pltpu.VMEM((256, 3 * INNER), BF16),
            pltpu.VMEM((256, WIDTH), F32),
            pltpu.VMEM((128, WIDTH), F32),
            pltpu.VMEM(frames.shape, BF16),
            pltpu.SemaphoreType.DMA,
        ],
        streamed=6,
    )(out_weight, mixed, out_grad, frames, head, tail, pos_row, gain, back_recv)
    merged = call(merge_kernel, shape((64, 8, 512), BF16))(pieces[0], *along_x, pieces[4], *along_y)
    last_recv = swap_all(jnp.concatenate([merged, small], axis=2))
    own = call(tm_sum_kernel, shape((16, 896), F32))(last_recv)
    across = flip(0, 2)(own)
    grad_qkv, grad_out, grad_conv, grad_gain = call(
        last_kernel,
        (shape((16, 1536), F32), shape((16, 512), F32), shape((16, 27), F32), shape((1, 16), F32)),
        [pltpu.VMEM((16, 2048), F32)],
    )(own, flip(0, 1)(own), across, flip(0, 1)(across))
    return block_out, grad_qkv, grad_out.T, grad_conv.T, grad_gain.reshape(16)


def solution(mesh):
    return jax.shard_map(
        body,
        mesh=mesh,
        in_specs=(
            P("clip", "tm", None, None),
            P(),
            P(),
            P(),
            P(),
            P(),
            P("clip", "tm", None, None),
        ),
        out_specs=(
            P("clip", "tm", None, None),
            P("tm", None),
            P(None, "tm"),
            P(None, "tm"),
            P("tm"),
        ),
        check_vma=False,
    )
```

```python
import jax
import jax.numpy as jnp
from jax import lax
from jax.experimental import pallas as pl
from jax.experimental.pallas import tpu as pltpu
from jax.sharding import PartitionSpec as P

HEADS = 8
HDIM = 64
GRID = 28
EPSILON = 1e-05
SCORE_SCALE = 0.125
F32 = jnp.float32
BF16 = jnp.bfloat16

WIDTH = 1024
INNER = HEADS * HDIM
VIS = 64
CHUNK = 256
STEPS = [(a, b) for a in (-1, 0, 1) for b in (-1, 0, 1)]
SIDES = [s for s in range(9) if s != 4]


def call(kernel, out_shape, scratch=(), limit=12, streamed=0, cost=None):
    def run(*args):
        def streaming(*refs):
            sources, refs = refs[:streamed], refs[streamed:]
            plain = len(refs) - streamed - 1
            buffers, sems = refs[plain : plain + streamed], refs[-1]
            copies = [
                pltpu.make_async_copy(source, buffer, sems.at[n])
                for n, (source, buffer) in enumerate(zip(sources, buffers))
            ]
            for copy in copies:
                copy.start()
            kernel(lambda n: copies[n].wait(), *buffers, *refs[:plain])

        extra = [pltpu.VMEM(x.shape, x.dtype) for x in args[:streamed]]
        specs = [pl.BlockSpec(memory_space=pltpu.HBM)] * streamed
        specs += [pl.BlockSpec(memory_space=pltpu.VMEM)] * (len(args) - streamed)
        return pl.pallas_call(
            streaming if streamed else kernel,
            out_shape=out_shape,
            in_specs=specs,
            out_specs=jax.tree.map(home, out_shape),
            scratch_shapes=list(scratch)
            + (extra + [pltpu.SemaphoreType.DMA((streamed,))] if streamed else []),
            compiler_params=pltpu.CompilerParams(vmem_limit_bytes=limit * 1024 * 1024),
            cost_estimate=cost,
            name=kernel.__name__,
        )(*[pltpu.with_memory_space_constraint(x, pltpu.HBM) for x in args[:streamed]], *args[streamed:])

    return run


def home(out):
    return pl.BlockSpec(memory_space=pltpu.VMEM if isinstance(out, jax.ShapeDtypeStruct) else pltpu.HBM)


def shape(dims, dtype):
    return jax.ShapeDtypeStruct(dims, dtype)


def mm(left, right):
    return jnp.dot(left, right, preferred_element_type=F32)


def mm_nt(left, right):
    return lax.dot_general(left, right, (((1,), (1,)), ((), ())), preferred_element_type=F32)


def mm_tn(left, right):
    return lax.dot_general(left, right, (((0,), (0,)), ((), ())), preferred_element_type=F32)


def pack_matrix():
    row = lax.broadcasted_iota(jnp.int32, (256, 256), 0)
    col = lax.broadcasted_iota(jnp.int32, (256, 256), 1)
    return jnp.where(((row & 7) << 5) + (row >> 3) == col, 1.0, 0.0).astype(BF16)


def unpack_matrix():
    row = lax.broadcasted_iota(jnp.int32, (256, 256), 0)
    col = lax.broadcasted_iota(jnp.int32, (256, 256), 1)
    return jnp.where(((row & 31) << 3) + (row >> 5) == col, 1.0, 0.0).astype(BF16)


def tap_rows(pos_row):
    pos = pos_row[...]
    key = pos + 36 * ((pos * 2341) >> 16)
    across = jnp.broadcast_to(key.astype(F32), (VIS, VIS))
    diff = across - jnp.transpose(across)
    mats = [jnp.where(diff == 64 * STEPS[s][0] + STEPS[s][1], 1.0, 0.0) for s in SIDES]
    return jnp.concatenate(mats, axis=0).astype(BF16)


def norm_parts(mixed):
    average = jnp.mean(mixed, axis=-1, keepdims=True)
    centred = mixed - average
    variance = jnp.mean(centred * centred, axis=-1, keepdims=True)
    inv_std = lax.rsqrt(variance + EPSILON)
    return centred * inv_std, inv_std


def frame_at(frames_ref, head_ref, tail_ref, c, u, cols):
    if u == 0:
        return head_ref[c, 0, :, cols]
    if u == 3:
        return tail_ref[c, 0, :, cols]
    return frames_ref[c, u - 1, :, cols]


def moved_at(taps, cells):
    moved = mm(taps, cells)
    out = [moved[64 * k : 64 * k + 64] for k in range(8)]
    out.insert(4, cells.astype(F32))
    return out


def pack(source, out_ref):
    matrix = pack_matrix()
    for b in range(2):
        rows = [source(h, ct, b) for h in range(2) for ct in range(4)]
        moved = mm(matrix, jnp.concatenate(rows, axis=0))
        out_ref[32 * b : 32 * b + 32] = moved.reshape(32, 8, moved.shape[-1]).astype(BF16)


def unpack(in_ref, sink):
    matrix = unpack_matrix()
    for b in range(2):
        block = in_ref[32 * b : 32 * b + 32]
        moved = mm(matrix, block.reshape(256, block.shape[-1])).astype(BF16)
        for h in range(2):
            for ct in range(4):
                at = 32 * (4 * h + ct)
                sink(h, ct, b, moved[at : at + 32])


def unpack_to(in_ref, out_ref):
    width = in_ref.shape[-1]

    def sink(h, ct, b, block):
        at = 64 * ct + 32 * b
        out_ref[at : at + 32, width * h : width * h + width] = block

    unpack(in_ref, sink)


def unpack_two(in_ref, left_ref, right_ref):
    def sink(h, ct, b, block):
        at = 64 * ct + 32 * b
        (left_ref, right_ref)[h][at : at + 32, :] = block

    unpack(in_ref, sink)


def local_kernel(ready, frames_ref, w_ref, pos_row, mixed_ref):
    taps = tap_rows(pos_row)
    ready(0)
    ready(1)

    @pl.loop(0, WIDTH // CHUNK)
    def _(n):
        cols = pl.ds(pl.multiple_of(n * CHUNK, CHUNK), CHUNK)
        w = w_ref[:, cols]
        for c in range(2):
            acc = [frames_ref[c, t, :, cols].astype(F32) for t in range(2)]
            for u in (1, 2):
                moved = moved_at(taps, frames_ref[c, u - 1, :, cols])
                for s in range(9):
                    for t in range(2):
                        at = 9 * (u - t) + s
                        acc[t] = acc[t] + w[at : at + 1] * moved[s]
            for t in range(2):
                at = 64 * (2 * c + t)
                mixed_ref[at : at + 64, cols] = acc[t]


def mix_kernel(
    ready, grad_ref, part_ref, head_ref, tail_ref, pos_row, w_ref, gain_ref,
    send_ref, kept_ref, mixed_ref, hidden_ref, sem,
):
    taps = tap_rows(pos_row)

    @pl.loop(0, WIDTH // CHUNK)
    def _(n):
        cols = pl.ds(pl.multiple_of(n * CHUNK, CHUNK), CHUNK)
        w = w_ref[:, cols]
        for c in range(2):
            for t, halo_ref in enumerate((head_ref, tail_ref)):
                moved = moved_at(taps, halo_ref[c, 0, :, cols])
                rows = slice(64 * (2 * c + t), 64 * (2 * c + t) + 64)
                acc = part_ref[rows, cols]
                for s in range(9):
                    at = 18 * t + s
                    acc = acc + w[at : at + 1] * moved[s]
                mixed_ref[rows, cols] = acc

    keep = pltpu.make_async_copy(mixed_ref, kept_ref, sem)
    keep.start()
    for k in range(8):
        rows = slice(32 * k, 32 * k + 32)
        normed, _ = norm_parts(mixed_ref[rows])
        hidden_ref[rows] = (normed * gain_ref[...]).astype(BF16)

    def source(h, ct, b):
        if h == 0:
            return hidden_ref[64 * ct + 32 * b : 64 * ct + 32 * b + 32, :]
        return grad_ref[ct // 2, ct % 2, 32 * b : 32 * b + 32, :]

    ready(0)
    pack(source, send_ref)
    keep.wait()


def attend_kernel(
    recv_ref, wqkv_ref, wout_ref,
    send_ref, hidden_ref, grad_ref, tok_ref, attn_ref,
    qkv_ref, up_ref, back_ref,
):
    unpack_two(recv_ref, hidden_ref, grad_ref)
    up_ref[...] = mm_nt(grad_ref[...], wout_ref[...]).astype(BF16)
    for n in range(3):
        cols = slice(512 * n, 512 * n + 512)
        qkv_ref[:, cols] = mm(hidden_ref[...], wqkv_ref[:, cols]).astype(BF16)

    low = lax.broadcasted_iota(jnp.int32, (128, 128), 1) < 64

    def halves(value):
        zero = jnp.zeros_like(value)
        return jnp.where(low, value, zero), jnp.where(low, zero, value)

    for c in range(2):
        rows = slice(128 * c, 128 * c + 128)
        pairs = [slice(128 * p, 128 * p + 128) for p in range(4)]
        query = [qkv_ref[rows, 128 * p : 128 * p + 128] for p in range(4)]
        key = [qkv_ref[rows, INNER + 128 * p : INNER + 128 * p + 128] for p in range(4)]
        value = [qkv_ref[rows, 2 * INNER + 128 * p : 2 * INNER + 128 * p + 128] for p in range(4)]
        upstream = [up_ref[rows, at] for at in pairs]
        queries = [halves(x) for x in query]
        upstreams = [halves(x) for x in upstream]
        heads = [(p, e) for p in range(4) for e in range(2)]
        scores = [mm_nt(queries[p][e], key[p]) * SCORE_SCALE for p, e in heads]
        d_soft = [mm_nt(upstreams[p][e], value[p]).astype(BF16).astype(F32) for p, e in heads]
        scores = [jnp.exp(x - jnp.max(x, axis=-1, keepdims=True)) for x in scores]
        soft = [x * (1.0 / jnp.sum(x, axis=-1, keepdims=True)) for x in scores]
        weights = [x.astype(BF16) for x in soft]
        inner = [jnp.sum(d * x, axis=-1, keepdims=True) for d, x in zip(d_soft, soft)]
        grads = [
            (x * (d - i) * SCORE_SCALE).astype(BF16) for d, x, i in zip(d_soft, soft, inner)
        ]
        for p in range(4):
            at = 128 * p
            both = slice(2 * p, 2 * p + 2)
            attn_ref[rows, at : at + 128] = mm(
                jnp.concatenate(weights[both], axis=1), jnp.concatenate(halves(value[p]), axis=0)
            ).astype(BF16)
            tok_ref[rows, at : at + 128] = mm(
                jnp.concatenate(grads[both], axis=1), jnp.concatenate(halves(key[p]), axis=0)
            ).astype(BF16)
            tok_ref[rows, INNER + at : INNER + at + 128] = mm_tn(
                jnp.concatenate(grads[both], axis=0), jnp.concatenate(queries[p], axis=0)
            ).astype(BF16)
            tok_ref[rows, 2 * INNER + at : 2 * INNER + at + 128] = mm_tn(
                jnp.concatenate(weights[both], axis=0), jnp.concatenate(upstreams[p], axis=0)
            ).astype(BF16)

    for n in range(2):
        cols = slice(512 * n, 512 * n + 512)
        back_ref[:, cols] = mm_nt(tok_ref[...], wqkv_ref[cols, :]).astype(BF16)
    back_ref[:, WIDTH:] = attn_ref[...]

    def source(h, ct, b):
        at = 64 * ct + 32 * b
        return back_ref[at : at + 32, 768 * h : 768 * h + 768]

    pack(source, send_ref)


def places():
    tm, clip = lax.axis_index("tm"), lax.axis_index("clip")
    return lax.rem(lax.div(tm, 8), 2), lax.div(tm, 16), lax.div(clip, 2), lax.rem(clip, 2)


def weight_half(hidden_ref, tok_ref, grad_ref, attn_ref, half, sink):
    @pl.when(half == 0)
    def _():
        turned = jnp.transpose(hidden_ref[...])
        for n in range(4):
            sink(256 * n, mm(turned, tok_ref[:, 256 * n : 256 * n + 256]))

    @pl.when(half == 1)
    def _():
        turned = jnp.transpose(hidden_ref[...])
        for n in range(2):
            sink(256 * n, mm(turned, tok_ref[:, 1024 + 256 * n : 1280 + 256 * n]))
        turned = jnp.transpose(grad_ref[...])
        for n in range(2):
            sink(512 + 256 * n, mm(turned, attn_ref[:, 256 * n : 256 * n + 256]))


def part_kernel(hidden_ref, tok_ref, grad_ref, attn_ref, give_ref):
    core = places()[3]

    def sink(at, value):
        give_ref[:, at : at + 256] = value.astype(BF16)

    weight_half(hidden_ref, tok_ref, grad_ref, attn_ref, 1 - core, sink)


def core_sum_kernel(hidden_ref, tok_ref, grad_ref, attn_ref, got_ref, *refs):
    piece_refs, both_ref = refs[:8], refs[8]
    x_lo, y, x_hi, core = places()

    def sink(at, value):
        both = value + got_ref[:, at : at + 256].astype(F32)
        both_ref[:, at : at + 256] = both.astype(BF16)

    weight_half(hidden_ref, tok_ref, grad_ref, attn_ref, core, sink)

    def part(at):
        return both_ref[:, pl.ds(pl.multiple_of(at, 128), 128)]

    for piece, (flip_lo, flip_hi) in enumerate(((0, 0), (1, 0), (0, 1), (1, 1))):
        lo = x_lo if flip_lo == 0 else 1 - x_lo
        hi = x_hi if flip_hi == 0 else 1 - x_hi
        piece_refs[piece][...] = part(256 * hi + 128 * lo)
    for k in range(4):
        piece_refs[4 + k][...] = part(512 + 128 * ((y + k) & 3))


def merge_kernel(*refs):
    out_ref = refs[-1]
    for side in range(2):
        a, b, c, d = (ref[...].astype(F32) for ref in refs[4 * side : 4 * side + 4])
        total = ((a + b) + (c + d)).reshape(64, 16, 128)
        for half in range(2):
            at = 256 * side + 128 * half
            out_ref[:, :, at : at + 128] = total[:, 8 * half : 8 * half + 8].astype(BF16)


def finish_kernel(
    ready, wout_ref, mixed_ref, grad_ref, frames_ref, head_ref, tail_ref, pos_row, gain_ref, recv_ref,
    out_ref, small_ref,
    back_ref, gm_ref, rows_ref, block_ref, sem,
):
    unpack_to(recv_ref, back_ref)
    gain = gain_ref[...]
    rows_ref[...] = jnp.zeros_like(rows_ref)
    ready(0)
    ready(1)
    for ct in range(4):
        at = slice(64 * ct, 64 * ct + 64)
        proj = mm(back_ref[at, WIDTH:], wout_ref[...])
        block_ref[ct // 2, ct % 2] = (mixed_ref[at] + proj).astype(BF16)
    write = pltpu.make_async_copy(block_ref, out_ref, sem)
    write.start()
    ready(2)
    gain_sum = jnp.zeros((8, WIDTH), F32)
    for k in range(8):
        rows = slice(32 * k, 32 * k + 32)
        normed, inv_std = norm_parts(mixed_ref[rows])
        grad_hidden = back_ref[rows, :WIDTH].astype(F32)
        prod = grad_hidden * normed
        gain_sum = gain_sum + jnp.sum(prod.reshape(4, 8, WIDTH), axis=0)
        scaled = grad_hidden * gain
        first = jnp.mean(scaled, axis=-1, keepdims=True)
        second = jnp.mean(prod * gain, axis=-1, keepdims=True)
        ct, half = k // 2, k % 2
        upstream = grad_ref[ct // 2, ct % 2, 32 * half : 32 * half + 32, :].astype(F32)
        gm_ref[rows] = inv_std * (scaled - first - normed * second) + upstream
    rows_ref[27:28, :] = jnp.sum(gain_sum, axis=0, keepdims=True)
    taps = tap_rows(pos_row)
    for n in (3, 4, 5):
        ready(n)

    @pl.loop(0, WIDTH // CHUNK)
    def _(n):
        cols = pl.ds(pl.multiple_of(n * CHUNK, CHUNK), CHUNK)
        acc = [jnp.zeros((8, CHUNK), F32) for _ in range(27)]
        for c in range(2):
            gm = [gm_ref[64 * (2 * c + t) : 64 * (2 * c + t) + 64, cols] for t in range(2)]
            for u in range(4):
                moved = moved_at(taps, frame_at(frames_ref, head_ref, tail_ref, c, u, cols))
                for s in range(9):
                    for t in range(2):
                        lag = u - t
                        if 0 <= lag <= 2:
                            prod = (gm[t] * moved[s]).reshape(8, 8, CHUNK)
                            acc[9 * lag + s] = acc[9 * lag + s] + jnp.sum(prod, axis=0)
        for at in range(27):
            rows_ref[at : at + 1, cols] = jnp.sum(acc[at], axis=0, keepdims=True)

    rows_ref[64:96, :] = rows_ref[0:32, :]
    turned = jnp.transpose(rows_ref[...]).reshape(64, 16, 128)
    left = lax.broadcasted_iota(jnp.int32, (64, 8, 128), 2) < 64
    small_ref[...] = jnp.where(left, turned[:, :8], turned[:, 8:]).astype(BF16)
    write.wait()


def tm_sum_kernel(recv_ref, out_ref):
    def over(first, last, at):
        total = recv_ref[first, :, at : at + 128].astype(F32)
        for src in range(first + 1, last):
            total = total + recv_ref[src, :, at : at + 128].astype(F32)
        return total

    for half in range(2):
        rows = slice(8 * half, 8 * half + 8)
        kept = [[over(16 * y + 8 * lo, 16 * y + 8 * lo + 8, 128 * half) for lo in range(2)] for y in range(4)]
        for lo in range(2):
            out_ref[rows, 128 * lo : 128 * lo + 128] = (kept[0][lo] + kept[1][lo]) + (kept[2][lo] + kept[3][lo])
        for y in range(4):
            at = 256 + 128 * y
            out_ref[rows, at : at + 128] = over(16 * y, 16 * y + 16, 256 + 128 * half)
    out_ref[:8, 768:] = over(0, 64, 512)
    out_ref[8:, 768:] = jnp.zeros((8, 128), F32)


def last_kernel(own_ref, core_ref, hi_ref, both_ref, qkv_ref, out_ref, conv_ref, gain_ref, full_ref):
    _, _, x_hi, core = places()
    mine = pl.multiple_of(1024 * core, 1024)
    other = pl.multiple_of(1024 - 1024 * core, 1024)
    here = pl.multiple_of(256 * x_hi, 256)
    there = pl.multiple_of(256 - 256 * x_hi, 256)
    full_ref[:, pl.ds(mine + here, 256)] = own_ref[:, :256]
    full_ref[:, pl.ds(mine + there, 256)] = hi_ref[:, :256]
    full_ref[:, pl.ds(other + here, 256)] = core_ref[:, :256]
    full_ref[:, pl.ds(other + there, 256)] = both_ref[:, :256]
    full_ref[:, pl.ds(mine + 512, 512)] = own_ref[:, 256:768] + hi_ref[:, 256:768]
    full_ref[:, pl.ds(other + 512, 512)] = core_ref[:, 256:768] + both_ref[:, 256:768]
    qkv_ref[...] = full_ref[:, :1536]
    out_ref[...] = full_ref[:, 1536:]
    small = (own_ref[:8, 768:] + core_ref[:8, 768:]) + (hi_ref[:8, 768:] + both_ref[:8, 768:])
    small = jnp.concatenate([small, pltpu.roll(small, 64, 1)], axis=0)
    conv_ref[...] = small[:, :27]
    padded = jnp.concatenate([small, jnp.zeros((112, 128), F32)], axis=0)
    gain_ref[...] = jnp.transpose(padded)[27:28, :16]


def flip(tm_bits, clip_bits):
    pairs = [(t * 4 + k, (t ^ tm_bits) * 4 + (k ^ clip_bits)) for t in range(64) for k in range(4)]
    return lambda value: lax.ppermute(value, ("tm", "clip"), pairs)


def swap_all(value):
    return lax.all_to_all(value, "tm", 0, 0, tiled=True)


def body(frames, vis_pos, conv_weight, norm_gain, qkv_weight, out_weight, out_grad):
    ends = lax.axis_size("tm") - 1
    head = lax.ppermute(frames[:, 1:], "tm", [(i, i + 1) for i in range(ends)])
    tail = lax.ppermute(frames[:, :1], "tm", [(i + 1, i) for i in range(ends)])
    pos_row = vis_pos.reshape(1, VIS)
    gain = norm_gain.reshape(1, WIDTH)
    local = call(local_kernel, shape((256, WIDTH), F32), streamed=2)(frames, conv_weight, pos_row)
    send, mixed = call(
        mix_kernel,
        (shape((64, 8, WIDTH), BF16), pltpu.HBM((256, WIDTH), F32)),
        [pltpu.VMEM((256, WIDTH), F32), pltpu.VMEM((256, WIDTH), BF16), pltpu.SemaphoreType.DMA],
        streamed=1,
    )(out_grad, local, head, tail, pos_row, conv_weight, gain)
    recv = swap_all(send)
    back, hidden, grad_tok, tok, attn = call(
        attend_kernel,
        (
            shape((64, 8, 768), BF16),
            shape((256, WIDTH), BF16),
            shape((256, WIDTH), BF16),
            shape((256, 3 * INNER), BF16),
            shape((256, INNER), BF16),
        ),
        [
            pltpu.VMEM((256, 3 * INNER), BF16),
            pltpu.VMEM((256, INNER), BF16),
            pltpu.VMEM((256, 3 * INNER), BF16),
        ],
        limit=16,
    )(recv, qkv_weight, out_weight)
    back_recv = swap_all(back)
    light = pl.CostEstimate(flops=1, bytes_accessed=1, transcendentals=0)
    terms = (hidden, tok, grad_tok, attn)
    give = call(part_kernel, shape((1024, 1024), BF16), cost=light)(*terms)
    got = flip(0, 1)(give)
    pieces = call(
        core_sum_kernel,
        (shape((1024, 128), BF16),) * 8,
        [pltpu.VMEM((1024, 1024), BF16)],
        cost=light,
    )(*terms, got)
    along_x = (flip(8, 0)(pieces[1]), flip(0, 2)(pieces[2]), flip(8, 2)(pieces[3]))
    along_y = [
        lax.ppermute(pieces[4 + k], "tm", [(i, (i + 16 * k) % 64) for i in range(64)]) for k in (1, 2, 3)
    ]
    block_out, small = call(
        finish_kernel,
        (pltpu.HBM(frames.shape, BF16), shape((64, 8, 128), BF16)),
        [
            pltpu.VMEM((256, 3 * INNER), BF16),
            pltpu.VMEM((256, WIDTH), F32),
            pltpu.VMEM((128, WIDTH), F32),
            pltpu.VMEM(frames.shape, BF16),
            pltpu.SemaphoreType.DMA,
        ],
        streamed=6,
    )(out_weight, mixed, out_grad, frames, head, tail, pos_row, gain, back_recv)
    merged = call(merge_kernel, shape((64, 8, 512), BF16))(pieces[0], *along_x, pieces[4], *along_y)
    last_recv = swap_all(jnp.concatenate([merged, small], axis=2))
    own = call(tm_sum_kernel, shape((16, 896), F32))(last_recv)
    across = flip(0, 2)(own)
    grad_qkv, grad_out, grad_conv, grad_gain = call(
        last_kernel,
        (shape((16, 1536), F32), shape((16, 512), F32), shape((16, 27), F32), shape((1, 16), F32)),
        [pltpu.VMEM((16, 2048), F32)],
    )(own, flip(0, 1)(own), across, flip(0, 1)(across))
    return block_out, grad_qkv, grad_out.T, grad_conv.T, grad_gain.reshape(16)


def solution(mesh):
    return jax.shard_map(
        body,
        mesh=mesh,
        in_specs=(
            P("clip", "tm", None, None),
            P(),
            P(),
            P(),
            P(),
            P(),
            P("clip", "tm", None, None),
        ),
        out_specs=(
            P("clip", "tm", None, None),
            P("tm", None),
            P(None, "tm"),
            P(None, "tm"),
            P("tm"),
        ),
        check_vma=False,
    )
```
